512 devices in a mesh: elem: 32 (over z, core), mode: 16 (over y, x).
Axes of the slice: x: 4, y: 4, z: 16, core: 2. Of those that a mesh axis runs over, the one named last changes fastest.
Arguments:
- adjoint: float32 [3, 256, 49, 4096], P(None, 'mode', None, 'elem'), may hold values from -2 to 2
- base_flow: float32 [3, 256, 49, 4096], P(None, 'mode', None, 'elem'), may hold values from -2 to 2
- metric: float32 [4, 49, 4096], P(None, None, 'elem'), may hold values from -1 to 1
- penalty: float32 [4, 7, 4096], P(None, None, 'elem'), may hold values from 0.5 to 4
- send_sides: int32 [32, 4, 32], P('elem'), may hold values from 0 to 512, as said below
- ext_index: int32 [4, 4096], P(None, 'elem'), may hold values from 0 to 640, as said below
Outputs:
- advect: float32 [3, 256, 49, 4096], P(None, 'mode', None, 'elem')
The draws below stay inside these ranges and needn't reach their ends.
Inputs may be any that keep to these rules, and one draw needn't show every extreme that they name: `send_sides`: entry [p, d, k] is a local side index s * 128 + e of partition p, sent in slot k of block d to partition p + o_d modulo 32 with o = (1, -1, 2, -2); the value 4 * 128 marks an empty slot. No side is sent twice. In every draw some partition fills all 32 slots of some block. `ext_index`: for side s of element e of partition p: a value below 512 is a local side of p; 512 + d * 32 + k is slot k of block d arriving from partition p - o_d; 640 means no neighbour. Pairings are mutual, and every sent side is read by its partner.
All inputs are finite; a program needn't handle non-finite values.
Results may differ from the reference program's by a relative error of at most 0.000098.
Values sent between devices are 32-bit elements; how exact they have to be, the bound alone decides.
No kernel may reach another device: no remote copies, remote signals or barrier semaphores. Data moves between devices by JAX's collectives and lax.ppermute only.
A program may use at most 128 MiB of HBM per device.

```python
import math
import jax
import jax.numpy as jnp
import numpy as np
from jax import lax

P_SIZE = 7
QP = 49
MODES = 256
E_DEV = 128
SLOTS = 32
ELEMS = 4096
N_ELEM = 32


def build_graph(key):
    side_count = 4 * E_DEV
    subkeys = jax.random.split(key, 4)
    orders = jax.vmap(lambda sub: jax.random.permutation(sub, side_count))(jax.random.split(subkeys[0], N_ELEM)).astype(jnp.int32)
    near_counts = jax.random.randint(subkeys[1], (N_ELEM,), SLOTS // 2, SLOTS + 1)
    full_at = jax.random.randint(subkeys[2], (), 0, N_ELEM)
    parts = jnp.arange(N_ELEM)
    near_counts = jnp.where(parts == full_at, SLOTS, near_counts)
    far_counts = jax.random.randint(subkeys[3], (N_ELEM,), SLOTS // 4, SLOTS // 2 + 1)
    counts = jnp.stack([near_counts, near_counts[(parts - 1) % N_ELEM], far_counts, far_counts[(parts - 2) % N_ELEM]], axis=1)
    slot_index = jnp.arange(SLOTS)
    reserved = orders[:, :4 * SLOTS].reshape(N_ELEM, 4, SLOTS)
    occupied = slot_index[None, None, :] < counts[:, :, None]
    sent_sides = jnp.where(occupied, reserved, side_count)
    partner = jnp.array([1, 0, 3, 2])
    arrival = side_count + partner[None, :, None] * SLOTS + slot_index[None, None, :]
    reserved_outer = jnp.where(occupied, arrival, side_count + 4 * SLOTS)
    remaining = jnp.arange(4 * SLOTS, side_count)
    remaining_outer = orders[:, remaining ^ 1]
    outer_pos = jnp.concatenate([reserved_outer.reshape(N_ELEM, 4 * SLOTS), remaining_outer], axis=1)
    inverse = jnp.argsort(orders, axis=1)
    outer_side = jnp.take_along_axis(outer_pos, inverse, axis=1)
    outer_index = jnp.transpose(outer_side.reshape(N_ELEM, 4, E_DEV), (1, 0, 2)).reshape(4, N_ELEM * E_DEV)
    return (sent_sides.astype(jnp.int32), outer_index.astype(jnp.int32))


def draw_send_sides(key, part):
    sent_sides, outer_index = build_graph(key)
    return sent_sides


def draw_ext_index(key, part):
    sent_sides, outer_index = build_graph(key)
    return outer_index


def shard_levels(key, extent, cuts, smallest, largest):
    factor_of, own = 1.0, jax.random.fold_in(key, 6)
    for dim, shards_of in cuts:
        draws = jnp.exp(jax.random.uniform(jax.random.fold_in(own, dim), (shards_of,), jnp.float32, smallest / len(cuts), largest / len(cuts)))
        factor_of = factor_of * jnp.repeat(draws, extent[dim] // shards_of).reshape([-1 if axis == dim else 1 for axis in range(len(extent))])
    return factor_of


def bell_draw(rng, dims, scale, limit, cuts=(), kind=jnp.bfloat16):
    loudness = shard_levels(rng, dims, cuts, -0.22, 0.18) if cuts else 1.0
    values = jax.random.normal(rng, dims, jnp.float32) * scale * loudness
    return jnp.minimum(jnp.maximum(values, -limit), limit).astype(kind)


def setup_inputs(seed: int = 0) -> dict:
    key_of = jax.random.split(jax.random.key(seed), 7)
    return {
        "adjoint": bell_draw(key_of[0], (3, MODES, QP, ELEMS), 0.3, 2.0, ((1, 16), (3, 32)), jnp.float32),
        "base_flow": bell_draw(key_of[1], (3, MODES, QP, ELEMS), 0.3, 2.0, ((1, 16), (3, 32)), jnp.float32),
        "metric": bell_draw(key_of[2], (4, QP, ELEMS), 0.2, 1.0, ((2, 32),), jnp.float32),
        "penalty": jnp.clip(jnp.exp(math.log(4.0) - 2.0794415 * jax.random.uniform(key_of[3], (4, P_SIZE, ELEMS), jnp.float32) ** shard_levels(key_of[3], (4, P_SIZE, ELEMS), ((2, 32),), -0.2, 0.2)), 0.5, 4.0),
        "send_sides": draw_send_sides(jax.random.fold_in(key_of[6], 71), 0),
        "ext_index": draw_ext_index(jax.random.fold_in(key_of[6], 71), 0),
    }


PRECISE = lax.Precision.HIGHEST
OFFSETS = (1, -1, 2, -2)


def legendre_pair(degree, position):
    previous = 1.0
    current = position
    for order_index in range(2, degree + 1):
        following = ((2 * order_index - 1) * position * current - (order_index - 1) * previous) / order_index
        previous = current
        current = following
    return current, previous


def lobatto_points(degree):
    node_list = []
    for point_index in range(degree + 1):
        estimate = -math.cos(math.pi * point_index / degree)
        for newton_step in range(60):
            current, previous = legendre_pair(degree, estimate)
            estimate = estimate - (estimate * current - previous) / ((degree + 1) * current)
        node_list.append(estimate)
    node_list[0] = -1.0
    node_list[degree] = 1.0
    return node_list


def lobatto_matrix(degree):
    lobatto_nodes = lobatto_points(degree)
    at_nodes = [legendre_pair(degree, value)[0] for value in lobatto_nodes]
    node_count = degree + 1
    matrix = np.zeros((node_count, node_count))
    for row_index in range(node_count):
        for col_index in range(node_count):
            if row_index != col_index:
                matrix[row_index, col_index] = at_nodes[row_index] / (at_nodes[col_index] * (lobatto_nodes[row_index] - lobatto_nodes[col_index]))
    matrix[0, 0] = -degree * (degree + 1) / 4.0
    matrix[degree, degree] = degree * (degree + 1) / 4.0
    return matrix


def element_tables(points):
    matrix = lobatto_matrix(points - 1)
    identity = np.eye(points)
    derive_first = np.kron(identity, matrix)
    derive_second = np.kron(matrix, identity)
    lift_table = np.zeros((points * points, 4 * points))
    final_index = points - 1
    for step_index in range(points):
        rim_points = (step_index, points * step_index + final_index, points * final_index + final_index - step_index, points * (final_index - step_index))
        for side_index in range(4):
            lift_table[rim_points[side_index], step_index * 4 + side_index] = 1.0
    return tuple(jnp.asarray(numeric).astype(jnp.float32) for numeric in (derive_first, derive_second, lift_table))


def fourier_tables(mode_count):
    planes = jnp.arange(mode_count, dtype=jnp.int32)[:, None]
    slot_index = jnp.arange(mode_count, dtype=jnp.int32)[None, :]
    wavenumber = slot_index // 2
    angles = ((wavenumber * planes) % mode_count).astype(jnp.float32) * (2.0 * math.pi / mode_count)
    nyquist = jnp.where(planes % 2 == 0, 1.0, -1.0).astype(jnp.float32)
    synthesis = jnp.where(slot_index % 2 == 1, -jnp.sin(angles), jnp.cos(angles))
    synthesis = jnp.where(slot_index == 1, nyquist, synthesis)
    weights = jnp.where(slot_index < 2, 1.0, 2.0).astype(jnp.float32) / mode_count
    analysis = jnp.transpose(synthesis * weights)
    rates = wavenumber.astype(jnp.float32) * (4.0 / mode_count)
    evens = synthesis[:, 0::2]
    odds = synthesis[:, 1::2]
    slope_table = jnp.stack([rates[:, 0::2] * odds, -rates[:, 0::2] * evens], axis=2).reshape(mode_count, mode_count)
    return synthesis, analysis, slope_table


def planar(fields, metric, derive_first, derive_second):
    first_slope = jnp.einsum('pq,fmqe->fmpe', derive_first, fields, precision=PRECISE)
    second_slope = jnp.einsum('pq,fmqe->fmpe', derive_second, fields, precision=PRECISE)
    return metric[0] * first_slope + metric[2] * second_slope, metric[1] * first_slope + metric[3] * second_slope


def combine(physical, east_slope, north_slope, span_slope):
    velocity = physical[:3]
    base_part = physical[3:]
    carried = base_part[0] * east_slope[:3] + base_part[1] * north_slope[:3] + base_part[2] * span_slope[:3]
    turned = jnp.stack([jnp.sum(velocity * gradient[3:], axis=0) for gradient in (east_slope, north_slope, span_slope)])
    return turned - carried


def global_penalty(adjoint, penalty, send_sides, ext_index, lift_table):
    components, mode_count, quad_points, elem_count = adjoint.shape
    points = penalty.shape[1]
    part_count = send_sides.shape[0]
    local_sides = 4 * E_DEV
    traces = jnp.einsum('qr,cmqe->cmre', lift_table, adjoint, precision=PRECISE)
    traces = traces.reshape(components, mode_count, points, 4, part_count, E_DEV)
    inner_traces = jnp.transpose(traces, (0, 1, 2, 4, 3, 5))
    ordered = inner_traces.reshape(components, mode_count, points, part_count * local_sides)
    padded = jnp.concatenate([ordered, jnp.zeros((components, mode_count, points, 1), jnp.float32)], axis=3)
    zero_at = part_count * local_sides
    parts = jnp.arange(part_count, dtype=jnp.int32)
    own_sides = parts[:, None] * local_sides + jnp.arange(local_sides, dtype=jnp.int32)[None, :]
    regions = []
    for direction, offset in enumerate(OFFSETS):
        source = (parts - offset) % part_count
        sent_sides = send_sides[source, direction]
        regions.append(jnp.where(sent_sides == local_sides, zero_at, source[:, None] * local_sides + sent_sides).astype(jnp.int32))
    lookup = jnp.concatenate([own_sides] + regions + [jnp.full((part_count, 1), zero_at, jnp.int32)], axis=1)
    chosen = jnp.transpose(ext_index.reshape(4, part_count, E_DEV), (1, 0, 2)).reshape(part_count, local_sides)
    global_index = jnp.take_along_axis(lookup, chosen.astype(jnp.int32), axis=1)
    outer = jnp.take(padded, global_index.reshape(-1), axis=3)[:, :, ::-1]
    outer = outer.reshape(components, mode_count, points, part_count, 4, E_DEV)
    weights = jnp.transpose(penalty.reshape(4, points, part_count, E_DEV), (1, 2, 0, 3))
    weighted = (outer - inner_traces) * weights
    weighted = jnp.transpose(weighted, (0, 1, 2, 4, 3, 5)).reshape(components, mode_count, points * 4, elem_count)
    return jnp.einsum('qr,cmre->cmqe', lift_table, weighted, precision=PRECISE)


def reference(adjoint, base_flow, metric, penalty, send_sides, ext_index):
    points = penalty.shape[1]
    synthesis, analysis, slope_table = fourier_tables(MODES)
    derive_first, derive_second, lift_table = element_tables(points)
    block_count = ELEMS // E_DEV

    def blocked(array):
        shaped = array.reshape(array.shape[:-1] + (block_count, E_DEV))
        return jnp.moveaxis(shaped, -2, 0)

    def one_block(inputs):
        velocity, base_part, geometry = inputs
        fields = jnp.concatenate([velocity, base_part], axis=0)
        physical = jnp.einsum('nm,fmqe->fnqe', synthesis, fields, precision=PRECISE)
        span_slope = jnp.einsum('nm,fmqe->fnqe', slope_table, fields, precision=PRECISE)
        east_slope, north_slope = planar(physical, geometry, derive_first, derive_second)
        product = combine(physical, east_slope, north_slope, span_slope)
        return jnp.einsum('mn,inqe->imqe', analysis, product, precision=PRECISE)

    pieces = lax.map(one_block, (blocked(adjoint), blocked(base_flow), blocked(metric)))
    volume = jnp.moveaxis(pieces, 0, -2).reshape(adjoint.shape)
    return volume + global_penalty(adjoint, penalty, send_sides, ext_index, lift_table)
```

```python
import math

import jax
import jax.numpy as jnp
import numpy as np
from jax import lax
from jax.experimental import pallas as pl
from jax.experimental.pallas import tpu as pltpu
from jax.sharding import PartitionSpec as P

MODES = 256
POINTS = 7
QUAD = 49
GROUPS = 16
NEAR = 8
ROWS = 6 * QUAD
FIELD_TILES = 37
BACK_ROWS = 3 * QUAD
BACK_TILES = 19
SLOTS = 32
OFFSETS = (1, -1, 2, -2)
TRACE_ROWS = 3 * POINTS * GROUPS
TRACE_LANES = 384
VMEM_LIMIT = 56 * 1024 * 1024


def legendre_pair(degree, position):
    previous = 1.0
    current = position
    for order_index in range(2, degree + 1):
        following = (
            (2 * order_index - 1) * position * current - (order_index - 1) * previous
        ) / order_index
        previous = current
        current = following
    return (current, previous)


def lobatto_points(degree):
    node_list = []
    for point_index in range(degree + 1):
        estimate = -math.cos(math.pi * point_index / degree)
        for newton_step in range(60):
            current, previous = legendre_pair(degree, estimate)
            estimate = estimate - (estimate * current - previous) / ((degree + 1) * current)
        node_list.append(estimate)
    node_list[0] = -1.0
    node_list[degree] = 1.0
    return node_list


def lobatto_matrix(degree):
    nodes = lobatto_points(degree)
    at_nodes = [legendre_pair(degree, value)[0] for value in nodes]
    count = degree + 1
    matrix = np.zeros((count, count))
    for row in range(count):
        for col in range(count):
            if row != col:
                matrix[row, col] = at_nodes[row] / (at_nodes[col] * (nodes[row] - nodes[col]))
    matrix[0, 0] = -degree * (degree + 1) / 4.0
    matrix[degree, degree] = degree * (degree + 1) / 4.0
    return matrix


def fourier_tables():
    planes = np.arange(MODES)[:, None]
    slot = np.arange(MODES)[None, :]
    wavenumber = slot // 2
    angles = (wavenumber * planes % MODES) * (2.0 * math.pi / MODES)
    synthesis = np.where(slot % 2 == 1, -np.sin(angles), np.cos(angles))
    synthesis = np.where(slot == 1, np.where(planes % 2 == 0, 1.0, -1.0), synthesis)
    weights = np.where(slot < 2, 1.0, 2.0) / MODES
    analysis = (synthesis * weights).T
    rates = wavenumber * (4.0 / MODES)
    slope = np.zeros((MODES, MODES))
    slope[:, 0::2] = rates[:, 0::2] * synthesis[:, 1::2]
    slope[:, 1::2] = -rates[:, 0::2] * synthesis[:, 0::2]
    return synthesis, analysis, slope


def halves(table):
    table = table.astype(np.float32)
    high = table.astype(jnp.bfloat16)
    low = (table - high.astype(np.float32)).astype(jnp.bfloat16)
    return high, low


def rim_point(side, step):
    last = POINTS - 1
    return (step, POINTS * step + last, POINTS * last + last - step, POINTS * (last - step))[side]


def swap_blocks(tiles, masks):
    turned = [pltpu.roll(tile, 16 * q, 1) if q else tile for q, tile in enumerate(tiles)]
    moved = [turned[-k % 8] for k in range(8)]
    for bit in range(3):
        moved = [jnp.where(masks[bit], moved[(k - (1 << bit)) % 8], moved[k]) for k in range(8)]
    return [pltpu.roll(tile, 128 - 16 * g, 1) if g else tile for g, tile in enumerate(moved)]


def block_masks():
    block = lax.broadcasted_iota(jnp.int32, (8, 128), 1) // 16
    return [(block & (1 << bit)) != 0 for bit in range(3)]


def split_two(value):
    high = value.astype(jnp.bfloat16)
    low = (value - high.astype(jnp.float32)).astype(jnp.bfloat16)
    return high, low


def split_three(value):
    high = value.astype(jnp.bfloat16)
    rest = value - high.astype(jnp.float32)
    middle = rest.astype(jnp.bfloat16)
    low = (rest - middle.astype(jnp.float32)).astype(jnp.bfloat16)
    return high, middle, low


def dot(left, right):
    return jnp.dot(left, right, preferred_element_type=jnp.float32)


def pack_kernel(adjoint_ref, base_ref, out_ref):
    def put(tile, block):
        out_ref[:, tile] = block.reshape(128, 128).T.reshape(GROUPS, NEAR, 128)

    for tile in range(FIELD_TILES):
        first, end = 8 * tile, min(8 * tile + 8, ROWS)
        parts = []
        if first < BACK_ROWS:
            parts.append(adjoint_ref[first : min(end, BACK_ROWS)])
        if end > BACK_ROWS:
            parts.append(base_ref[max(first, BACK_ROWS) - BACK_ROWS : end - BACK_ROWS])
        if 8 * tile + 8 > end:
            parts.append(base_ref[: 8 * tile + 8 - end])
        put(tile, parts[0] if len(parts) == 1 else jnp.concatenate(parts, axis=0))


def derive_line(values, odd_table, even_table, centre):
    sums = [values[k] + values[6 - k] for k in range(3)]
    differences = [values[k] - values[6 - k] for k in range(3)]
    even = [
        sum(float(odd_table[i, j]) * differences[j] for j in range(1, 3))
        + float(odd_table[i, 0]) * differences[0]
        for i in range(4)
    ]
    odd = [
        (float(even_table[i, 0]) * sums[0] + float(even_table[i, 1]) * sums[1])
        + (float(even_table[i, 2]) * sums[2] + float(centre[i]) * values[3])
        for i in range(3)
    ]
    return (
        [even[i] + odd[i] for i in range(3)]
        + [even[3]]
        + [even[i] - odd[i] for i in (2, 1, 0)]
    )


def main_kernel(
    in_ref,
    metric_ref,
    synth_high_ref,
    synth_low_ref,
    back_high_ref,
    back_low_ref,
    out_ref,
    high,
    low,
    plane,
    first,
    second,
    product,
    coefficient,
):
    masks = block_masks()

    @pl.loop(0, FIELD_TILES)
    def _(tile):
        rows = pl.ds(pl.multiple_of(tile * 64, 64), 64)
        for half in range(2):
            swapped = swap_blocks([in_ref[8 * half + k, tile] for k in range(8)], masks)
            upper, lower = split_two(jnp.concatenate(swapped, axis=0))
            high[rows, pl.ds(128 * half, 128)] = upper
            low[rows, pl.ds(128 * half, 128)] = lower

    block = FIELD_TILES * 16

    @pl.loop(0, 4)
    def _(step):
        rows = pl.ds(pl.multiple_of(step * block, 16), block)
        upper = high[rows, :]
        plane[rows, :] = (
            dot(upper, synth_high_ref[...])
            + dot(low[rows, :], synth_high_ref[...])
            + dot(upper, synth_low_ref[...])
        )

    matrix = lobatto_matrix(POINTS - 1)
    mirrored = matrix[:, ::-1]
    odd_table = (matrix - mirrored)[:4, :3] / 2.0
    even_table = (matrix + mirrored)[:3, :3] / 2.0
    centre = matrix[:3, 3]

    @pl.loop(0, 6)
    def _(field):
        def at(point):
            return pl.ds(pl.multiple_of(field * (QUAD * 8) + point * 8, 8), 8)

        for half in range(2):
            lanes = pl.ds(128 * half, 128)
            for line in range(POINTS):
                for stride, base, target in ((1, 7 * line, first), (7, line, second)):
                    values = [plane[at(base + stride * k), lanes] for k in range(POINTS)]
                    for k, slope in enumerate(derive_line(values, odd_table, even_table, centre)):
                        target[at(base + stride * k), lanes] = slope

    @pl.loop(0, QUAD)
    def _(point):
        east_first, north_first, east_second, north_second = (metric_ref[k, point] for k in range(4))

        def at(field):
            return pl.ds(pl.multiple_of(field * (QUAD * 8) + point * 8, 8), 8)

        for half in range(2):
            lanes = pl.ds(128 * half, 128)
            span = pl.ds(MODES + 128 * half, 128)
            speed = [plane[at(k), lanes] for k in range(3)]
            base = [plane[at(3 + k), lanes] for k in range(3)]
            along = sum(speed[k] * first[at(3 + k), lanes] for k in range(3))
            across = sum(speed[k] * second[at(3 + k), lanes] for k in range(3))
            turned = (
                east_first * along + east_second * across,
                north_first * along + north_second * across,
                sum(speed[k] * plane[at(3 + k), span] for k in range(3)),
            )
            flow_first = base[0] * east_first + base[1] * north_first
            flow_second = base[0] * east_second + base[1] * north_second
            for k in range(3):
                carried = (
                    flow_first * first[at(k), lanes]
                    + flow_second * second[at(k), lanes]
                    + base[2] * plane[at(k), span]
                )
                product[at(k), lanes] = turned[k] - carried

    product[BACK_ROWS * 8 :, :] = jnp.zeros((BACK_TILES * 64 - BACK_ROWS * 8, MODES), jnp.float32)
    back_block = BACK_TILES * 32

    @pl.loop(0, 2)
    def _(step):
        rows = pl.ds(pl.multiple_of(step * back_block, 32), back_block)
        upper, lower = split_two(product[rows, :])
        coefficient[rows, :] = (
            dot(upper, back_high_ref[...])
            + dot(lower, back_high_ref[...])
            + dot(upper, back_low_ref[...])
        )

    @pl.loop(0, BACK_TILES)
    def _(tile):
        for half in range(2):
            lanes = pl.ds(128 * half, 128)
            pieces = [
                coefficient[pl.ds(pl.multiple_of(tile * 64 + 8 * k, 8), 8), lanes] for k in range(8)
            ]
            for k, swapped in enumerate(swap_blocks(pieces, masks)):
                out_ref[8 * half + k, tile] = swapped


def traces_of(adjoint_ref):
    return jnp.concatenate(
        [
            jnp.concatenate(
                [adjoint_ref[component * QUAD + rim_point(side, step)] for side in range(4)], axis=1
            )
            for component in range(3)
            for step in range(POINTS)
        ],
        axis=0,
    )


def send_kernel(adjoint_ref, sides_ref, *out_refs):
    traces = traces_of(adjoint_ref)
    chosen = lax.broadcasted_iota(jnp.int32, (512, 4 * SLOTS), 0) == sides_ref[...]
    chosen = jnp.where(chosen, 1.0, 0.0).astype(jnp.bfloat16)
    outgoing = sum(dot(part, chosen) for part in split_three(traces))
    padding = jnp.zeros((TRACE_LANES - TRACE_ROWS, 128), jnp.float32)
    outgoing = jnp.concatenate([outgoing, padding], axis=0).T
    for direction, out_ref in enumerate(out_refs):
        out_ref[...] = outgoing[direction * SLOTS : (direction + 1) * SLOTS]


def metric_kernel(group_ref, metric_ref, out_ref, turned):
    turned[...] = jnp.concatenate(
        [metric_ref[...], jnp.zeros((256 - 4 * QUAD, 128), jnp.float32)], axis=0
    ).T
    own = turned[pl.ds(pl.multiple_of(group_ref[0] * NEAR, NEAR), NEAR), :]
    for index in range(4 * QUAD):
        out_ref[index] = jnp.broadcast_to(own[:, index : index + 1], (NEAR, 128))


def jump_kernel(adjoint_ref, index_ref, penalty_ref, *refs):
    received_refs, out_ref = refs[:4], refs[4]
    traces = traces_of(adjoint_ref)
    received = jnp.concatenate([ref[...] for ref in received_refs], axis=0).T[:TRACE_ROWS]
    index = index_ref[...]
    where_local = lax.broadcasted_iota(jnp.int32, (512, 128), 0)
    where_far = lax.broadcasted_iota(jnp.int32, (128, 128), 0) + 512
    local_parts = split_three(traces)
    far_parts = split_three(received)
    for side in range(4):
        wanted = index[side : side + 1]
        near = jnp.where(where_local == wanted, 1.0, 0.0).astype(jnp.bfloat16)
        far = jnp.where(where_far == wanted, 1.0, 0.0).astype(jnp.bfloat16)
        outer = sum(dot(part, near) for part in local_parts) + sum(
            dot(part, far) for part in far_parts
        )
        for component in range(3):
            for step in range(POINTS):
                row = (component * POINTS + step) * GROUPS
                far_row = (component * POINTS + 6 - step) * GROUPS
                weight = penalty_ref[side * POINTS + step : side * POINTS + step + 1]
                inner = adjoint_ref[component * QUAD + rim_point(side, step)]
                jump = outer[far_row : far_row + GROUPS] - inner
                out_ref[(component * POINTS + step) * 4 + side] = weight * jump


def unpack_kernel(in_ref, jump_ref, out_ref):
    sides_at = {}
    for side in range(4):
        for step in range(POINTS):
            sides_at.setdefault(rim_point(side, step), []).append((side, step))
    for tile in range(BACK_TILES):
        block = in_ref[:, tile].reshape(128, 128).T
        for k in range(8):
            row = 8 * tile + k
            if row >= BACK_ROWS:
                break
            component, point = divmod(row, QUAD)
            value = block[16 * k : 16 * k + 16]
            for side, step in sides_at.get(point, ()):
                value = value + jump_ref[(component * POINTS + step) * 4 + side]
            out_ref[row] = value


def call(kernel, shapes, *args, scratch=(), scalars=0, flops=0):
    vmem = pl.BlockSpec(memory_space=pltpu.VMEM)
    smem = pl.BlockSpec(memory_space=pltpu.SMEM)
    many = isinstance(shapes, list)
    outs = [jax.ShapeDtypeStruct(s, jnp.float32) for s in (shapes if many else [shapes])]
    moved = sum(int(np.prod(a.shape)) * a.dtype.itemsize for a in args)
    moved += sum(int(np.prod(o.shape)) * 4 for o in outs)
    return pl.pallas_call(
        kernel,
        out_shape=outs if many else outs[0],
        in_specs=[smem] * scalars + [vmem] * (len(args) - scalars),
        out_specs=[vmem] * len(outs) if many else vmem,
        scratch_shapes=list(scratch),
        compiler_params=pltpu.CompilerParams(vmem_limit_bytes=VMEM_LIMIT),
        cost_estimate=pl.CostEstimate(flops=flops, bytes_accessed=moved, transcendentals=0),
    )(*args)


def passed_along(block, axis, distance):
    count = lax.axis_size(axis)
    return lax.ppermute(block, axis, [((i - distance) % count, i) for i in range(count)])


def shards(adjoint, base_flow, metric, penalty, send_sides, ext_index):
    synthesis, analysis, slope = fourier_tables()
    synth_high, synth_low = halves(np.concatenate([synthesis, slope], axis=0).T)
    back_high, back_low = halves(analysis.T)
    natural = jnp.transpose(adjoint, (0, 2, 1, 3)).reshape(BACK_ROWS, GROUPS, 128)
    base = jnp.transpose(base_flow, (0, 2, 1, 3)).reshape(BACK_ROWS, GROUPS, 128)
    group = lax.axis_index("mode").reshape(1)

    packed = call(pack_kernel, (GROUPS, FIELD_TILES, NEAR, 128), natural, base)
    arrived = lax.all_to_all(packed, "mode", split_axis=0, concat_axis=0, tiled=True)

    outgoing = call(
        send_kernel, [(SLOTS, TRACE_LANES)] * 4, natural, send_sides.reshape(1, 4 * SLOTS)
    )
    received = [passed_along(block, "elem", o) for block, o in zip(outgoing, OFFSETS)]
    own_metric = call(
        metric_kernel,
        (4 * QUAD, NEAR, 128),
        group,
        metric.reshape(4 * QUAD, 128),
        scratch=[pltpu.VMEM((128, 256), jnp.float32)],
        scalars=1,
    ).reshape(4, QUAD, NEAR, 128)

    field_rows, back_rows = FIELD_TILES * 64, BACK_TILES * 64
    coefficients = call(
        main_kernel,
        (GROUPS, BACK_TILES, NEAR, 128),
        arrived,
        own_metric,
        jnp.asarray(synth_high),
        jnp.asarray(synth_low),
        jnp.asarray(back_high),
        jnp.asarray(back_low),
        scratch=[
            pltpu.VMEM((field_rows, MODES), jnp.bfloat16),
            pltpu.VMEM((field_rows, MODES), jnp.bfloat16),
            pltpu.VMEM((field_rows, 2 * MODES), jnp.float32),
            pltpu.VMEM((ROWS * 8, MODES), jnp.float32),
            pltpu.VMEM((ROWS * 8, MODES), jnp.float32),
            pltpu.VMEM((back_rows, MODES), jnp.float32),
            pltpu.VMEM((back_rows, MODES), jnp.float32),
        ],
    )
    returned = lax.all_to_all(coefficients, "mode", split_axis=0, concat_axis=0, tiled=True)
    jumps = call(
        jump_kernel,
        (84, GROUPS, 128),
        natural,
        ext_index,
        penalty.reshape(4 * POINTS, 128),
        *received,
    )
    out = call(unpack_kernel, (BACK_ROWS, GROUPS, 128), returned, jumps)
    return jnp.transpose(out.reshape(3, QUAD, GROUPS, 128), (0, 2, 1, 3))


def solution(mesh):
    placed = (
        P(None, "mode", None, "elem"),
        P(None, "mode", None, "elem"),
        P(None, None, "elem"),
        P(None, None, "elem"),
        P("elem", None, None),
        P(None, "elem"),
    )
    return jax.shard_map(
        shards, mesh=mesh, in_specs=placed, out_specs=P(None, "mode", None, "elem"), check_vma=False
    )
```

```python
import math

import jax
import jax.numpy as jnp
import numpy as np
from jax import lax
from jax.experimental import pallas as pl
from jax.experimental.pallas import tpu as pltpu
from jax.sharding import PartitionSpec as P

MODES = 256
POINTS = 7
QUAD = 49
GROUPS = 16
NEAR = 8
ROWS = 6 * QUAD
FIELD_TILES = 37
BACK_ROWS = 3 * QUAD
BACK_TILES = 19
SLOTS = 32
OFFSETS = (1, -1, 2, -2)
TRACE_ROWS = 3 * POINTS * GROUPS
TRACE_LANES = 384
MEBI = 1024 * 1024


def legendre_pair(degree, position):
    previous = 1.0
    current = position
    for order_index in range(2, degree + 1):
        following = (
            (2 * order_index - 1) * position * current - (order_index - 1) * previous
        ) / order_index
        previous = current
        current = following
    return (current, previous)


def lobatto_points(degree):
    node_list = []
    for point_index in range(degree + 1):
        estimate = -math.cos(math.pi * point_index / degree)
        for newton_step in range(60):
            current, previous = legendre_pair(degree, estimate)
            estimate = estimate - (estimate * current - previous) / ((degree + 1) * current)
        node_list.append(estimate)
    node_list[0] = -1.0
    node_list[degree] = 1.0
    return node_list


def lobatto_matrix(degree):
    nodes = lobatto_points(degree)
    at_nodes = [legendre_pair(degree, value)[0] for value in nodes]
    count = degree + 1
    matrix = np.zeros((count, count))
    for row in range(count):
        for col in range(count):
            if row != col:
                matrix[row, col] = at_nodes[row] / (at_nodes[col] * (nodes[row] - nodes[col]))
    matrix[0, 0] = -degree * (degree + 1) / 4.0
    matrix[degree, degree] = degree * (degree + 1) / 4.0
    return matrix


def fourier_tables():
    planes = np.arange(MODES)[:, None]
    slot = np.arange(MODES)[None, :]
    wavenumber = slot // 2
    angles = (wavenumber * planes % MODES) * (2.0 * math.pi / MODES)
    synthesis = np.where(slot % 2 == 1, -np.sin(angles), np.cos(angles))
    synthesis = np.where(slot == 1, np.where(planes % 2 == 0, 1.0, -1.0), synthesis)
    weights = np.where(slot < 2, 1.0, 2.0) / MODES
    analysis = (synthesis * weights).T
    rates = wavenumber * (4.0 / MODES)
    slope = np.zeros((MODES, MODES))
    slope[:, 0::2] = rates[:, 0::2] * synthesis[:, 1::2]
    slope[:, 1::2] = -rates[:, 0::2] * synthesis[:, 0::2]
    return synthesis, analysis, slope


def stacked(table):
    table = table.astype(np.float32)
    high = table.astype(jnp.bfloat16)
    low = (table - high.astype(np.float32)).astype(jnp.bfloat16)
    return np.concatenate([high, high, low], axis=0)


def rim_point(side, step):
    last = POINTS - 1
    return (step, POINTS * step + last, POINTS * last + last - step, POINTS * (last - step))[side]


def barrel(turned, masks):
    moved = [turned[-k % 8] for k in range(8)]
    for bit in range(3):
        moved = [jnp.where(masks[bit], moved[(k - (1 << bit)) % 8], moved[k]) for k in range(8)]
    return moved


def gather_blocks(turned, masks):
    return [
        pltpu.roll(tile, 128 - 16 * g, 1) if g else tile
        for g, tile in enumerate(barrel(turned, masks))
    ]


def scatter_blocks(tiles, masks):
    return barrel([pltpu.roll(tile, 16 * q, 1) if q else tile for q, tile in enumerate(tiles)], masks)


def block_masks():
    block = lax.broadcasted_iota(jnp.int32, (8, 128), 1) // 16
    return [(block & (1 << bit)) != 0 for bit in range(3)]


def split_two(value):
    high = value.astype(jnp.bfloat16)
    low = (value - high.astype(jnp.float32)).astype(jnp.bfloat16)
    return high, low


def split_three(value):
    high = value.astype(jnp.bfloat16)
    rest = value - high.astype(jnp.float32)
    middle = rest.astype(jnp.bfloat16)
    low = (rest - middle.astype(jnp.float32)).astype(jnp.bfloat16)
    return high, middle, low


def dot(left, right):
    return jnp.dot(left, right, preferred_element_type=jnp.float32)


def pack_kernel(group_ref, adjoint_ref, base_ref, out_ref):
    turn = group_ref[0] % 8
    order = [lax.rem(k - turn + 8, 8) for k in range(8)]

    def put(tile, source, first):
        block = jnp.concatenate([source[first + k] for k in order], axis=0)
        out_ref[:, tile] = block.T.reshape(GROUPS, NEAR, 128)

    @pl.loop(0, 18, unroll=3)
    def _(tile):
        put(tile, adjoint_ref, 8 * tile)

    @pl.loop(0, 17)
    def _(tile):
        put(19 + tile, base_ref, 8 * tile + 5)

    for tile, first in ((18, 144), (36, 288)):
        rows = []
        for k in order:
            row = jnp.minimum(first + k, ROWS - 1)
            inside = adjoint_ref[jnp.minimum(row, BACK_ROWS - 1)]
            outside = base_ref[jnp.maximum(row - BACK_ROWS, 0)]
            rows.append(jnp.where(row < BACK_ROWS, inside, outside))
        out_ref[:, tile] = jnp.concatenate(rows, axis=0).T.reshape(GROUPS, NEAR, 128)


def derive_line(values, odd_table, even_table, centre):
    sums = [values[k] + values[6 - k] for k in range(3)]
    differences = [values[k] - values[6 - k] for k in range(3)]
    even = [
        sum(float(odd_table[i, j]) * differences[j] for j in range(1, 3))
        + float(odd_table[i, 0]) * differences[0]
        for i in range(4)
    ]
    odd = [
        (float(even_table[i, 0]) * sums[0] + float(even_table[i, 1]) * sums[1])
        + (float(even_table[i, 2]) * sums[2] + float(centre[i]) * values[3])
        for i in range(3)
    ]
    return (
        [even[i] + odd[i] for i in range(3)]
        + [even[3]]
        + [even[i] - odd[i] for i in (2, 1, 0)]
    )


def main_kernel(
    in_ref,
    metric_ref,
    synth_ref,
    back_ref,
    jump_ref,
    out_ref,
    high,
    low,
    plane,
    first,
    second,
    product,
    coefficient,
):
    masks = block_masks()

    def gather(tile):
        rows = pl.ds(pl.multiple_of(tile * 64, 64), 64)
        for half in range(2):
            swapped = gather_blocks([in_ref[8 * half + k, tile] for k in range(8)], masks)
            upper, lower = split_two(jnp.concatenate(swapped, axis=0))
            high[rows, pl.ds(128 * half, 128)] = upper
            low[rows, pl.ds(128 * half, 128)] = lower

    pl.loop(0, FIELD_TILES - 1, unroll=4)(gather)
    gather(FIELD_TILES - 1)

    block = FIELD_TILES * 16

    @pl.loop(0, 4)
    def _(step):
        rows = pl.ds(pl.multiple_of(step * block, 16), block)
        upper = high[rows, :]
        parts = jnp.concatenate([upper, low[rows, :], upper], axis=1)
        plane[rows, :] = dot(parts, synth_ref[...])

    matrix = lobatto_matrix(POINTS - 1)
    mirrored = matrix[:, ::-1]
    odd_table = (matrix - mirrored)[:4, :3] / 2.0
    even_table = (matrix + mirrored)[:3, :3] / 2.0
    centre = matrix[:3, 3]

    @pl.loop(0, 6)
    def _(field):
        def at(point):
            return pl.ds(pl.multiple_of(field * (QUAD * 8) + point * 8, 8), 8)

        for half in range(2):
            lanes = pl.ds(128 * half, 128)
            for line in range(POINTS):
                for stride, base, target in ((1, 7 * line, first), (7, line, second)):
                    values = [plane[at(base + stride * k), lanes] for k in range(POINTS)]
                    for k, slope in enumerate(derive_line(values, odd_table, even_table, centre)):
                        target[at(base + stride * k), lanes] = slope

    @pl.loop(0, QUAD)
    def _(point):
        east_first, north_first, east_second, north_second = (metric_ref[k, point] for k in range(4))

        def at(field):
            return pl.ds(pl.multiple_of(field * (QUAD * 8) + point * 8, 8), 8)

        for half in range(2):
            lanes = pl.ds(128 * half, 128)
            span = pl.ds(MODES + 128 * half, 128)
            speed = [plane[at(k), lanes] for k in range(3)]
            base = [plane[at(3 + k), lanes] for k in range(3)]
            along = sum(speed[k] * first[at(3 + k), lanes] for k in range(3))
            across = sum(speed[k] * second[at(3 + k), lanes] for k in range(3))
            turned = (
                east_first * along + east_second * across,
                north_first * along + north_second * across,
                sum(speed[k] * plane[at(3 + k), span] for k in range(3)),
            )
            flow_first = base[0] * east_first + base[1] * north_first
            flow_second = base[0] * east_second + base[1] * north_second
            for k in range(3):
                carried = (
                    flow_first * first[at(k), lanes]
                    + flow_second * second[at(k), lanes]
                    + base[2] * plane[at(k), span]
                )
                product[at(k), lanes] = turned[k] - carried

    product[BACK_ROWS * 8 :, :] = jnp.zeros((BACK_TILES * 64 - BACK_ROWS * 8, MODES), jnp.float32)
    back_block = BACK_TILES * 32

    @pl.loop(0, 2)
    def _(step):
        rows = pl.ds(pl.multiple_of(step * back_block, 32), back_block)
        upper, lower = split_two(product[rows, :])
        parts = jnp.concatenate([upper, lower, upper], axis=1)
        coefficient[rows, :] = dot(parts, back_ref[...])

    def scatter(tile):
        for half in range(2):
            lanes = pl.ds(128 * half, 128)
            pieces = [
                coefficient[pl.ds(pl.multiple_of(tile * 64 + 8 * k, 8), 8), lanes] for k in range(8)
            ]
            for k, swapped in enumerate(scatter_blocks(pieces, masks)):
                out_ref[8 * half + k, tile] = swapped

    pl.loop(0, BACK_TILES - 1, unroll=3)(scatter)
    scatter(BACK_TILES - 1)


def traces_of(adjoint_ref):
    return jnp.concatenate(
        [
            jnp.concatenate(
                [adjoint_ref[component * QUAD + rim_point(side, step)] for side in range(4)], axis=1
            )
            for component in range(3)
            for step in range(POINTS)
        ],
        axis=0,
    )


def send_kernel(adjoint_ref, sides_ref, *out_refs):
    traces = traces_of(adjoint_ref)
    chosen = lax.broadcasted_iota(jnp.int32, (512, 4 * SLOTS), 0) == sides_ref[...]
    chosen = jnp.where(chosen, 1.0, 0.0).astype(jnp.bfloat16)
    outgoing = sum(dot(part, chosen) for part in split_three(traces))
    padding = jnp.zeros((TRACE_LANES - TRACE_ROWS, 128), jnp.float32)
    outgoing = jnp.concatenate([outgoing, padding], axis=0).T
    for direction, out_ref in enumerate(out_refs):
        out_ref[...] = outgoing[direction * SLOTS : (direction + 1) * SLOTS]


def metric_kernel(group_ref, metric_ref, out_ref, turned):
    turned[...] = jnp.concatenate(
        [metric_ref[...], jnp.zeros((256 - 4 * QUAD, 128), jnp.float32)], axis=0
    ).T
    own = turned[pl.ds(pl.multiple_of(group_ref[0] * NEAR, NEAR), NEAR), :]
    for index in range(4 * QUAD):
        out_ref[index] = jnp.broadcast_to(own[:, index : index + 1], (NEAR, 128))


def jump_kernel(adjoint_ref, index_ref, penalty_ref, *refs):
    received_refs, out_ref = refs[:4], refs[4]
    traces = traces_of(adjoint_ref)
    received = jnp.concatenate([ref[...] for ref in received_refs], axis=0).T[:TRACE_ROWS]
    index = index_ref[...]
    where_local = lax.broadcasted_iota(jnp.int32, (512, 128), 0)
    where_far = lax.broadcasted_iota(jnp.int32, (128, 128), 0) + 512
    local_parts = split_three(traces)
    far_parts = split_three(received)
    for side in range(4):
        wanted = index[side : side + 1]
        near = jnp.where(where_local == wanted, 1.0, 0.0).astype(jnp.bfloat16)
        far = jnp.where(where_far == wanted, 1.0, 0.0).astype(jnp.bfloat16)
        outer = sum(dot(part, near) for part in local_parts) + sum(
            dot(part, far) for part in far_parts
        )
        for component in range(3):
            for step in range(POINTS):
                row = (component * POINTS + step) * GROUPS
                far_row = (component * POINTS + 6 - step) * GROUPS
                weight = penalty_ref[side * POINTS + step : side * POINTS + step + 1]
                inner = adjoint_ref[component * QUAD + rim_point(side, step)]
                jump = outer[far_row : far_row + GROUPS] - inner
                out_ref[(component * POINTS + step) * 4 + side] = weight * jump


def unpack_kernel(group_ref, in_ref, jump_ref, out_ref):
    turn = group_ref[0] % 8

    def place(tile, count):
        block = in_ref[:, tile].reshape(128, 128).T
        for k in range(8):
            row = 8 * tile + lax.rem(k - turn + 8, 8)

            def store(row=row, k=k):
                out_ref[row] = block[16 * k : 16 * k + 16]

            if count == 8:
                store()
            else:
                pl.when(row < BACK_ROWS)(store)

    pl.loop(0, BACK_TILES - 1, unroll=3)(lambda tile: place(tile, 8))
    place(BACK_TILES - 1, BACK_ROWS % 8)
    sides_at = {}
    for side in range(4):
        for step in range(POINTS):
            sides_at.setdefault(rim_point(side, step), []).append((side, step))

    @pl.loop(0, 3)
    def _(component):
        for point, sides in sides_at.items():
            value = out_ref[component * QUAD + point]
            for side, step in sides:
                value = value + jump_ref[component * 4 * POINTS + step * 4 + side]
            out_ref[component * QUAD + point] = value


def call(kernel, shapes, *args, scratch=(), scalars=0, unread=0, grant=12):
    vmem = pl.BlockSpec(memory_space=pltpu.VMEM)
    smem = pl.BlockSpec(memory_space=pltpu.SMEM)
    anywhere = pl.BlockSpec(memory_space=pl.ANY)
    many = isinstance(shapes, list)
    outs = [jax.ShapeDtypeStruct(s, jnp.float32) for s in (shapes if many else [shapes])]
    moved = sum(int(np.prod(a.shape)) * a.dtype.itemsize for a in args)
    moved += sum(int(np.prod(o.shape)) * 4 for o in outs)
    return pl.pallas_call(
        kernel,
        out_shape=outs if many else outs[0],
        in_specs=[smem] * scalars + [vmem] * (len(args) - scalars - unread) + [anywhere] * unread,
        out_specs=[vmem] * len(outs) if many else vmem,
        scratch_shapes=list(scratch),
        compiler_params=pltpu.CompilerParams(vmem_limit_bytes=grant * MEBI),
        cost_estimate=pl.CostEstimate(flops=0, bytes_accessed=moved, transcendentals=0),
    )(*args)


def passed_along(block, axis, distance):
    count = lax.axis_size(axis)
    return lax.ppermute(block, axis, [((i - distance) % count, i) for i in range(count)])


def shards(adjoint, base_flow, metric, penalty, send_sides, ext_index):
    synthesis, analysis, slope = fourier_tables()
    synth = stacked(np.concatenate([synthesis, slope], axis=0).T)
    back = stacked(analysis.T)
    natural = jnp.transpose(adjoint, (0, 2, 1, 3)).reshape(BACK_ROWS, GROUPS, 128)
    base = jnp.transpose(base_flow, (0, 2, 1, 3)).reshape(BACK_ROWS, GROUPS, 128)
    group = lax.axis_index("mode").reshape(1)

    packed = call(pack_kernel, (GROUPS, FIELD_TILES, NEAR, 128), group, natural, base, scalars=1)
    arrived = lax.all_to_all(packed, "mode", split_axis=0, concat_axis=0, tiled=True)

    outgoing = call(
        send_kernel, [(SLOTS, TRACE_LANES)] * 4, natural, send_sides.reshape(1, 4 * SLOTS)
    )
    received = [passed_along(block, "elem", o) for block, o in zip(outgoing, OFFSETS)]
    own_metric = call(
        metric_kernel,
        (4 * QUAD, NEAR, 128),
        group,
        metric.reshape(4 * QUAD, 128),
        scratch=[pltpu.VMEM((128, 256), jnp.float32)],
        scalars=1,
    ).reshape(4, QUAD, NEAR, 128)
    jumps = call(
        jump_kernel,
        (84, GROUPS, 128),
        natural,
        ext_index,
        penalty.reshape(4 * POINTS, 128),
        *received,
    )

    field_rows, back_rows = FIELD_TILES * 64, BACK_TILES * 64
    coefficients = call(
        main_kernel,
        (GROUPS, BACK_TILES, NEAR, 128),
        arrived,
        own_metric,
        jnp.asarray(synth),
        jnp.asarray(back),
        jumps,
        scratch=[
            pltpu.VMEM((field_rows, MODES), jnp.bfloat16),
            pltpu.VMEM((field_rows, MODES), jnp.bfloat16),
            pltpu.VMEM((field_rows, 2 * MODES), jnp.float32),
            pltpu.VMEM((ROWS * 8, MODES), jnp.float32),
            pltpu.VMEM((ROWS * 8, MODES), jnp.float32),
            pltpu.VMEM((back_rows, MODES), jnp.float32),
            pltpu.VMEM((back_rows, MODES), jnp.float32),
        ],
        unread=1,
        grant=28,
    )
    returned = lax.all_to_all(coefficients, "mode", split_axis=0, concat_axis=0, tiled=True)
    out = call(unpack_kernel, (BACK_ROWS, GROUPS, 128), group, returned, jumps, scalars=1)
    return jnp.transpose(out.reshape(3, QUAD, GROUPS, 128), (0, 2, 1, 3))


def solution(mesh):
    placed = (
        P(None, "mode", None, "elem"),
        P(None, "mode", None, "elem"),
        P(None, None, "elem"),
        P(None, None, "elem"),
        P("elem", None, None),
        P(None, "elem"),
    )
    return jax.shard_map(
        shards, mesh=mesh, in_specs=placed, out_specs=P(None, "mode", None, "elem"), check_vma=False
    )
```

```python
import math

import jax
import jax.numpy as jnp
import numpy as np
from jax import lax
from jax.experimental import pallas as pl
from jax.experimental.pallas import tpu as pltpu
from jax.sharding import PartitionSpec as P

MODES = 256
POINTS = 7
QUAD = 49
GROUPS = 16
NEAR = 8
ROWS = 6 * QUAD
FIELD_TILES = 37
BACK_ROWS = 3 * QUAD
BACK_TILES = 19
SLOTS = 32
OFFSETS = (1, -1, 2, -2)
TRACE_ROWS = 3 * POINTS * GROUPS
TRACE_LANES = 384
MEBI = 1024 * 1024


def legendre_pair(degree, position):
    previous = 1.0
    current = position
    for order_index in range(2, degree + 1):
        following = (
            (2 * order_index - 1) * position * current - (order_index - 1) * previous
        ) / order_index
        previous = current
        current = following
    return (current, previous)


def lobatto_points(degree):
    node_list = []
    for point_index in range(degree + 1):
        estimate = -math.cos(math.pi * point_index / degree)
        for newton_step in range(60):
            current, previous = legendre_pair(degree, estimate)
            estimate = estimate - (estimate * current - previous) / ((degree + 1) * current)
        node_list.append(estimate)
    node_list[0] = -1.0
    node_list[degree] = 1.0
    return node_list


def lobatto_matrix(degree):
    nodes = lobatto_points(degree)
    at_nodes = [legendre_pair(degree, value)[0] for value in nodes]
    count = degree + 1
    matrix = np.zeros((count, count))
    for row in range(count):
        for col in range(count):
            if row != col:
                matrix[row, col] = at_nodes[row] / (at_nodes[col] * (nodes[row] - nodes[col]))
    matrix[0, 0] = -degree * (degree + 1) / 4.0
    matrix[degree, degree] = degree * (degree + 1) / 4.0
    return matrix


def fourier_tables():
    planes = np.arange(MODES)[:, None]
    slot = np.arange(MODES)[None, :]
    wavenumber = slot // 2
    angles = (wavenumber * planes % MODES) * (2.0 * math.pi / MODES)
    synthesis = np.where(slot % 2 == 1, -np.sin(angles), np.cos(angles))
    synthesis = np.where(slot == 1, np.where(planes % 2 == 0, 1.0, -1.0), synthesis)
    weights = np.where(slot < 2, 1.0, 2.0) / MODES
    analysis = (synthesis * weights).T
    rates = wavenumber * (4.0 / MODES)
    slope = np.zeros((MODES, MODES))
    slope[:, 0::2] = rates[:, 0::2] * synthesis[:, 1::2]
    slope[:, 1::2] = -rates[:, 0::2] * synthesis[:, 0::2]
    return synthesis, analysis, slope


def stacked(table):
    table = table.astype(np.float32)
    high = table.astype(jnp.bfloat16)
    low = (table - high.astype(np.float32)).astype(jnp.bfloat16)
    return np.concatenate([high, low], axis=0)


def rim_point(side, step):
    last = POINTS - 1
    return (step, POINTS * step + last, POINTS * last + last - step, POINTS * (last - step))[side]


def barrel(turned, masks):
    moved = [turned[-k % 8] for k in range(8)]
    for bit in range(3):
        moved = [jnp.where(masks[bit], moved[(k - (1 << bit)) % 8], moved[k]) for k in range(8)]
    return moved


def gather_blocks(turned, masks):
    return [
        pltpu.roll(tile, 128 - 16 * g, 1) if g else tile
        for g, tile in enumerate(barrel(turned, masks))
    ]


def scatter_blocks(tiles, masks):
    return barrel([pltpu.roll(tile, 16 * q, 1) if q else tile for q, tile in enumerate(tiles)], masks)


def block_masks():
    block = lax.broadcasted_iota(jnp.int32, (8, 128), 1) // 16
    return [(block & (1 << bit)) != 0 for bit in range(3)]


def split_two(value):
    high = value.astype(jnp.bfloat16)
    low = (value - high.astype(jnp.float32)).astype(jnp.bfloat16)
    return high, low


def split_three(value):
    high = value.astype(jnp.bfloat16)
    rest = value - high.astype(jnp.float32)
    middle = rest.astype(jnp.bfloat16)
    low = (rest - middle.astype(jnp.float32)).astype(jnp.bfloat16)
    return high, middle, low


def dot(left, right):
    return jnp.dot(left, right, preferred_element_type=jnp.float32)


FIELD_CUTS = (0, 48, 96, BACK_ROWS)
PACK_GROUPS = (0, 6, 12, 18, 24, 30, FIELD_TILES)


def pack_kernel(group_ref, adjoint_ref, base_ref, out_ref, fields, packed, in_sems, out_sems):
    arrivals = []
    for source, offset in ((adjoint_ref, 0), (base_ref, BACK_ROWS)):
        for first, end in zip(FIELD_CUTS, FIELD_CUTS[1:]):
            arrivals.append(
                pltpu.make_async_copy(
                    source.at[pl.ds(first, end - first)],
                    fields.at[pl.ds(offset + first, end - first)],
                    in_sems.at[len(arrivals)],
                )
            )
            arrivals[-1].start()
    fields[ROWS:] = jnp.zeros((8 * FIELD_TILES - ROWS, GROUPS, 128), jnp.float32)
    turn = group_ref[0] % 8
    order = [lax.rem(k - turn + 8, 8) for k in range(8)]
    departures = []
    for number, (first, end) in enumerate(zip(PACK_GROUPS, PACK_GROUPS[1:])):
        arrivals[number].wait()
        for tile in range(first, end):
            block = jnp.concatenate([fields[8 * tile + k] for k in order], axis=0)
            packed[:, tile] = block.T.reshape(GROUPS, NEAR, 128)
        departures.append(
            pltpu.make_async_copy(
                packed.at[:, pl.ds(first, end - first)],
                out_ref.at[:, pl.ds(first, end - first)],
                out_sems.at[number],
            )
        )
        departures[-1].start()
    for departure in departures:
        departure.wait()


def derive_line(values, odd_table, even_table, centre):
    sums = [values[k] + values[6 - k] for k in range(3)]
    differences = [values[k] - values[6 - k] for k in range(3)]
    even = [
        sum(float(odd_table[i, j]) * differences[j] for j in range(1, 3))
        + float(odd_table[i, 0]) * differences[0]
        for i in range(4)
    ]
    odd = [
        (float(even_table[i, 0]) * sums[0] + float(even_table[i, 1]) * sums[1])
        + (float(even_table[i, 2]) * sums[2] + float(centre[i]) * values[3])
        for i in range(3)
    ]
    return (
        [even[i] + odd[i] for i in range(3)]
        + [even[3]]
        + [even[i] - odd[i] for i in (2, 1, 0)]
    )


def main_kernel(
    in_ref,
    metric_ref,
    synth_ref,
    back_ref,
    jump_ref,
    out_ref,
    synth,
    back,
    table_sems,
    high,
    low,
    plane,
    first,
    second,
    product,
    coefficient,
):
    masks = block_masks()
    tables = []
    for source, target in ((synth_ref, synth), (back_ref, back)):
        for place, part in enumerate((0, 0, 1)):
            tables.append(
                pltpu.make_async_copy(
                    source.at[pl.ds(MODES * part, MODES)],
                    target.at[pl.ds(MODES * place, MODES)],
                    table_sems.at[len(tables)],
                )
            )
            tables[-1].start()

    def gather(tile):
        rows = pl.ds(pl.multiple_of(tile * 64, 64), 64)
        for half in range(2):
            swapped = gather_blocks([in_ref[8 * half + k, tile] for k in range(8)], masks)
            upper, lower = split_two(jnp.concatenate(swapped, axis=0))
            high[rows, pl.ds(128 * half, 128)] = upper
            low[rows, pl.ds(128 * half, 128)] = lower

    pl.loop(0, FIELD_TILES - 1, unroll=6)(gather)
    gather(FIELD_TILES - 1)
    for table in tables:
        table.wait()

    block = FIELD_TILES * 32

    @pl.loop(0, 2)
    def _(step):
        rows = pl.ds(pl.multiple_of(step * block, 16), block)
        upper = high[rows, :]
        parts = jnp.concatenate([upper, low[rows, :], upper], axis=1)
        plane[rows, :] = dot(parts, synth[...])

    matrix = lobatto_matrix(POINTS - 1)
    mirrored = matrix[:, ::-1]
    odd_table = (matrix - mirrored)[:4, :3] / 2.0
    even_table = (matrix + mirrored)[:3, :3] / 2.0
    centre = matrix[:3, 3]

    @pl.loop(0, 6)
    def _(field):
        def at(point):
            return pl.ds(pl.multiple_of(field * (QUAD * 8) + point * 8, 8), 8)

        for half in range(2):
            lanes = pl.ds(128 * half, 128)
            for line in range(POINTS):
                for stride, base, target in ((1, 7 * line, first), (7, line, second)):
                    values = [plane[at(base + stride * k), lanes] for k in range(POINTS)]
                    for k, slope in enumerate(derive_line(values, odd_table, even_table, centre)):
                        target[at(base + stride * k), lanes] = slope

    @pl.loop(0, QUAD)
    def _(point):
        east_first, north_first, east_second, north_second = (metric_ref[k, point] for k in range(4))

        def at(field):
            return pl.ds(pl.multiple_of(field * (QUAD * 8) + point * 8, 8), 8)

        for half in range(2):
            lanes = pl.ds(128 * half, 128)
            span = pl.ds(MODES + 128 * half, 128)
            speed = [plane[at(k), lanes] for k in range(3)]
            base = [plane[at(3 + k), lanes] for k in range(3)]
            along = sum(speed[k] * first[at(3 + k), lanes] for k in range(3))
            across = sum(speed[k] * second[at(3 + k), lanes] for k in range(3))
            turned = (
                east_first * along + east_second * across,
                north_first * along + north_second * across,
                sum(speed[k] * plane[at(3 + k), span] for k in range(3)),
            )
            flow_first = base[0] * east_first + base[1] * north_first
            flow_second = base[0] * east_second + base[1] * north_second
            for k in range(3):
                carried = (
                    flow_first * first[at(k), lanes]
                    + flow_second * second[at(k), lanes]
                    + base[2] * plane[at(k), span]
                )
                product[at(k), lanes] = turned[k] - carried

    product[BACK_ROWS * 8 :, :] = jnp.zeros((BACK_TILES * 64 - BACK_ROWS * 8, MODES), jnp.float32)
    upper, lower = split_two(product[...])
    parts = jnp.concatenate([upper, lower, upper], axis=1)
    coefficient[...] = dot(parts, back[...])

    def scatter(tile):
        for half in range(2):
            lanes = pl.ds(128 * half, 128)
            pieces = [
                coefficient[pl.ds(pl.multiple_of(tile * 64 + 8 * k, 8), 8), lanes] for k in range(8)
            ]
            for k, swapped in enumerate(scatter_blocks(pieces, masks)):
                out_ref[8 * half + k, tile] = swapped

    pl.loop(0, BACK_TILES - 1, unroll=3)(scatter)
    scatter(BACK_TILES - 1)


def traces_of(adjoint_ref):
    return jnp.concatenate(
        [
            jnp.concatenate(
                [adjoint_ref[component * QUAD + rim_point(side, step)] for side in range(4)], axis=1
            )
            for component in range(3)
            for step in range(POINTS)
        ],
        axis=0,
    )


def send_kernel(adjoint_ref, sides_ref, *out_refs):
    traces = traces_of(adjoint_ref)
    chosen = lax.broadcasted_iota(jnp.int32, (512, 4 * SLOTS), 0) == sides_ref[...]
    chosen = jnp.where(chosen, 1.0, 0.0).astype(jnp.bfloat16)
    outgoing = sum(dot(part, chosen) for part in split_three(traces))
    padding = jnp.zeros((TRACE_LANES - TRACE_ROWS, 128), jnp.float32)
    outgoing = jnp.concatenate([outgoing, padding], axis=0).T
    for direction, out_ref in enumerate(out_refs):
        out_ref[...] = outgoing[direction * SLOTS : (direction + 1) * SLOTS]


def metric_kernel(group_ref, metric_ref, out_ref, turned):
    turned[...] = jnp.concatenate(
        [metric_ref[...], jnp.zeros((256 - 4 * QUAD, 128), jnp.float32)], axis=0
    ).T
    own = turned[pl.ds(pl.multiple_of(group_ref[0] * NEAR, NEAR), NEAR), :]
    for index in range(4 * QUAD):
        out_ref[index] = jnp.broadcast_to(own[:, index : index + 1], (NEAR, 128))


def jump_kernel(adjoint_ref, index_ref, penalty_ref, *refs):
    received_refs, out_ref = refs[:4], refs[4]
    traces = traces_of(adjoint_ref)
    received = jnp.concatenate([ref[...] for ref in received_refs], axis=0).T[:TRACE_ROWS]
    index = index_ref[...]
    where_local = lax.broadcasted_iota(jnp.int32, (512, 128), 0)
    where_far = lax.broadcasted_iota(jnp.int32, (128, 128), 0) + 512
    local_parts = split_three(traces)
    far_parts = split_three(received)
    for side in range(4):
        wanted = index[side : side + 1]
        near = jnp.where(where_local == wanted, 1.0, 0.0).astype(jnp.bfloat16)
        far = jnp.where(where_far == wanted, 1.0, 0.0).astype(jnp.bfloat16)
        outer = sum(dot(part, near) for part in local_parts) + sum(
            dot(part, far) for part in far_parts
        )
        for component in range(3):
            for step in range(POINTS):
                row = (component * POINTS + step) * GROUPS
                far_row = (component * POINTS + 6 - step) * GROUPS
                weight = penalty_ref[side * POINTS + step : side * POINTS + step + 1]
                inner = adjoint_ref[component * QUAD + rim_point(side, step)]
                jump = outer[far_row : far_row + GROUPS] - inner
                out_ref[(component * POINTS + step) * 4 + side] = weight * jump


BACK_GROUPS = (0, 7, 13, BACK_TILES)


def unpack_kernel(group_ref, in_ref, jump_ref, out_ref, advect, sems):
    turn = group_ref[0] % 8
    sides_at = {}
    for side in range(4):
        for step in range(POINTS):
            sides_at.setdefault(rim_point(side, step), []).append((side, step))
    departures = []
    for component in range(3):
        for tile in range(BACK_GROUPS[component], BACK_GROUPS[component + 1]):
            block = in_ref[:, tile].reshape(128, 128).T
            for k in range(8):
                row = 8 * tile + lax.rem(k - turn + 8, 8)
                advect[row] = block[16 * k : 16 * k + 16]
        first = component * QUAD
        for point, sides in sides_at.items():
            value = advect[first + point]
            for side, step in sides:
                value = value + jump_ref[(component * POINTS + step) * 4 + side]
            advect[first + point] = value
        departures.append(
            pltpu.make_async_copy(
                advect.at[pl.ds(first, QUAD)], out_ref.at[pl.ds(first, QUAD)], sems.at[component]
            )
        )
        departures[-1].start()
    for departure in departures:
        departure.wait()


def call(kernel, shapes, *args, places=None, into=pltpu.VMEM, scratch=(), grant=12):
    spaces = {"v": pltpu.VMEM, "h": pltpu.HBM, "s": pltpu.SMEM, "a": pl.ANY}
    places = places or "v" * len(args)
    many = isinstance(shapes, list)
    if into is pltpu.HBM:
        outs = [pltpu.HBM(s, jnp.float32) for s in (shapes if many else [shapes])]
    else:
        outs = [jax.ShapeDtypeStruct(s, jnp.float32) for s in (shapes if many else [shapes])]
    moved = sum(int(np.prod(a.shape)) * a.dtype.itemsize for a in args)
    moved += sum(int(np.prod(o.shape)) * 4 for o in outs)
    args = [
        pltpu.with_memory_space_constraint(a, pltpu.HBM) if p == "h" else a
        for a, p in zip(args, places)
    ]
    out_spec = pl.BlockSpec(memory_space=into)
    return pl.pallas_call(
        kernel,
        out_shape=outs if many else outs[0],
        in_specs=[pl.BlockSpec(memory_space=spaces[p]) for p in places],
        out_specs=[out_spec] * len(outs) if many else out_spec,
        scratch_shapes=list(scratch),
        compiler_params=pltpu.CompilerParams(vmem_limit_bytes=grant * MEBI),
        cost_estimate=pl.CostEstimate(flops=0, bytes_accessed=moved, transcendentals=0),
    )(*args)


def passed_along(block, axis, distance):
    count = lax.axis_size(axis)
    return lax.ppermute(block, axis, [((i - distance) % count, i) for i in range(count)])


def shards(adjoint, base_flow, metric, penalty, send_sides, ext_index):
    synthesis, analysis, slope = fourier_tables()
    synth = stacked(np.concatenate([synthesis, slope], axis=0).T)
    back = stacked(analysis.T)
    natural = jnp.transpose(adjoint, (0, 2, 1, 3)).reshape(BACK_ROWS, GROUPS, 128)
    base = jnp.transpose(base_flow, (0, 2, 1, 3)).reshape(BACK_ROWS, GROUPS, 128)
    group = lax.axis_index("mode").reshape(1)

    packed = call(
        pack_kernel,
        (GROUPS, FIELD_TILES, NEAR, 128),
        group,
        natural,
        base,
        places="shh",
        into=pltpu.HBM,
        scratch=[
            pltpu.VMEM((8 * FIELD_TILES, GROUPS, 128), jnp.float32),
            pltpu.VMEM((GROUPS, FIELD_TILES, NEAR, 128), jnp.float32),
            pltpu.SemaphoreType.DMA((6,)),
            pltpu.SemaphoreType.DMA((6,)),
        ],
    )
    arrived = lax.all_to_all(packed, "mode", split_axis=0, concat_axis=0, tiled=True)

    outgoing = call(
        send_kernel, [(SLOTS, TRACE_LANES)] * 4, natural, send_sides.reshape(1, 4 * SLOTS)
    )
    received = [passed_along(block, "elem", o) for block, o in zip(outgoing, OFFSETS)]
    own_metric = call(
        metric_kernel,
        (4 * QUAD, NEAR, 128),
        group,
        metric.reshape(4 * QUAD, 128),
        places="sv",
        scratch=[pltpu.VMEM((128, 256), jnp.float32)],
    ).reshape(4, QUAD, NEAR, 128)
    jumps = call(
        jump_kernel,
        (84, GROUPS, 128),
        natural,
        ext_index,
        penalty.reshape(4 * POINTS, 128),
        *received,
    )

    field_rows, back_rows = FIELD_TILES * 64, BACK_TILES * 64
    coefficients = call(
        main_kernel,
        (GROUPS, BACK_TILES, NEAR, 128),
        arrived,
        own_metric,
        jnp.asarray(synth),
        jnp.asarray(back),
        jumps,
        places="vvhha",
        scratch=[
            pltpu.VMEM((3 * MODES, 2 * MODES), jnp.bfloat16),
            pltpu.VMEM((3 * MODES, MODES), jnp.bfloat16),
            pltpu.SemaphoreType.DMA((6,)),
            pltpu.VMEM((field_rows, MODES), jnp.bfloat16),
            pltpu.VMEM((field_rows, MODES), jnp.bfloat16),
            pltpu.VMEM((field_rows, 2 * MODES), jnp.float32),
            pltpu.VMEM((ROWS * 8, MODES), jnp.float32),
            pltpu.VMEM((ROWS * 8, MODES), jnp.float32),
            pltpu.VMEM((back_rows, MODES), jnp.float32),
            pltpu.VMEM((back_rows, MODES), jnp.float32),
        ],
        grant=28,
    )
    returned = lax.all_to_all(coefficients, "mode", split_axis=0, concat_axis=0, tiled=True)
    out = call(
        unpack_kernel,
        (BACK_ROWS, GROUPS, 128),
        group,
        returned,
        jumps,
        places="svv",
        into=pltpu.HBM,
        scratch=[
            pltpu.VMEM((8 * BACK_TILES, GROUPS, 128), jnp.float32),
            pltpu.SemaphoreType.DMA((3,)),
        ],
    )
    return jnp.transpose(out.reshape(3, QUAD, GROUPS, 128), (0, 2, 1, 3))


def solution(mesh):
    placed = (
        P(None, "mode", None, "elem"),
        P(None, "mode", None, "elem"),
        P(None, None, "elem"),
        P(None, None, "elem"),
        P("elem", None, None),
        P(None, "elem"),
    )
    return jax.shard_map(
        shards, mesh=mesh, in_specs=placed, out_specs=P(None, "mode", None, "elem"), check_vma=False
    )
```

```python
import math

import jax
import jax.numpy as jnp
import numpy as np
from jax import lax
from jax.experimental import pallas as pl
from jax.experimental.pallas import tpu as pltpu
from jax.sharding import PartitionSpec as P

MODES = 256
POINTS = 7
QUAD = 49
GROUPS = 16
NEAR = 8
ROWS = 6 * QUAD
FIELD_TILES = 37
BACK_ROWS = 3 * QUAD
BACK_TILES = 19
SLOTS = 32
OFFSETS = (1, -1, 2, -2)
TRACE_ROWS = 3 * POINTS * GROUPS
TRACE_LANES = 384
MEBI = 1024 * 1024


def legendre_pair(degree, position):
    previous = 1.0
    current = position
    for order_index in range(2, degree + 1):
        following = (
            (2 * order_index - 1) * position * current - (order_index - 1) * previous
        ) / order_index
        previous = current
        current = following
    return (current, previous)


def lobatto_points(degree):
    node_list = []
    for point_index in range(degree + 1):
        estimate = -math.cos(math.pi * point_index / degree)
        for newton_step in range(60):
            current, previous = legendre_pair(degree, estimate)
            estimate = estimate - (estimate * current - previous) / ((degree + 1) * current)
        node_list.append(estimate)
    node_list[0] = -1.0
    node_list[degree] = 1.0
    return node_list


def lobatto_matrix(degree):
    nodes = lobatto_points(degree)
    at_nodes = [legendre_pair(degree, value)[0] for value in nodes]
    count = degree + 1
    matrix = np.zeros((count, count))
    for row in range(count):
        for col in range(count):
            if row != col:
                matrix[row, col] = at_nodes[row] / (at_nodes[col] * (nodes[row] - nodes[col]))
    matrix[0, 0] = -degree * (degree + 1) / 4.0
    matrix[degree, degree] = degree * (degree + 1) / 4.0
    return matrix


def fourier_tables():
    planes = np.arange(MODES)[:, None]
    slot = np.arange(MODES)[None, :]
    wavenumber = slot // 2
    angles = (wavenumber * planes % MODES) * (2.0 * math.pi / MODES)
    synthesis = np.where(slot % 2 == 1, -np.sin(angles), np.cos(angles))
    synthesis = np.where(slot == 1, np.where(planes % 2 == 0, 1.0, -1.0), synthesis)
    weights = np.where(slot < 2, 1.0, 2.0) / MODES
    analysis = (synthesis * weights).T
    rates = wavenumber * (4.0 / MODES)
    slope = np.zeros((MODES, MODES))
    slope[:, 0::2] = rates[:, 0::2] * synthesis[:, 1::2]
    slope[:, 1::2] = -rates[:, 0::2] * synthesis[:, 0::2]
    return synthesis, analysis, slope


def stacked(table):
    table = table.astype(np.float32)
    high = table.astype(jnp.bfloat16)
    low = (table - high.astype(np.float32)).astype(jnp.bfloat16)
    return np.concatenate([high, low], axis=0)


def rim_point(side, step):
    last = POINTS - 1
    return (step, POINTS * step + last, POINTS * last + last - step, POINTS * (last - step))[side]


def barrel(turned, masks):
    moved = [turned[-k % 8] for k in range(8)]
    for bit in range(3):
        moved = [jnp.where(masks[bit], moved[(k - (1 << bit)) % 8], moved[k]) for k in range(8)]
    return moved


def gather_blocks(turned, masks):
    return [
        pltpu.roll(tile, 128 - 16 * g, 1) if g else tile
        for g, tile in enumerate(barrel(turned, masks))
    ]


def scatter_blocks(tiles, masks):
    return barrel([pltpu.roll(tile, 16 * q, 1) if q else tile for q, tile in enumerate(tiles)], masks)


def block_masks():
    block = lax.broadcasted_iota(jnp.int32, (8, 128), 1) // 16
    return [(block & (1 << bit)) != 0 for bit in range(3)]


def split_two(value):
    high = value.astype(jnp.bfloat16)
    low = (value - high.astype(jnp.float32)).astype(jnp.bfloat16)
    return high, low


def split_three(value):
    high = value.astype(jnp.bfloat16)
    rest = value - high.astype(jnp.float32)
    middle = rest.astype(jnp.bfloat16)
    low = (rest - middle.astype(jnp.float32)).astype(jnp.bfloat16)
    return high, middle, low


def dot(left, right):
    return jnp.dot(left, right, preferred_element_type=jnp.float32)


FIELD_CUTS = (0, 48, 96, BACK_ROWS)
PACK_GROUPS = (0, 6, 12, 18, 24, 30, FIELD_TILES)


def pack_kernel(group_ref, adjoint_ref, base_ref, out_ref, fields, packed, in_sems, out_sems):
    arrivals = []
    for source, offset in ((adjoint_ref, 0), (base_ref, BACK_ROWS)):
        for first, end in zip(FIELD_CUTS, FIELD_CUTS[1:]):
            arrivals.append(
                pltpu.make_async_copy(
                    source.at[pl.ds(first, end - first)],
                    fields.at[pl.ds(offset + first, end - first)],
                    in_sems.at[len(arrivals)],
                )
            )
            arrivals[-1].start()
    fields[ROWS:] = jnp.zeros((8 * FIELD_TILES - ROWS, GROUPS, 128), jnp.float32)
    turn = group_ref[0] % 8
    order = [lax.rem(k - turn + 8, 8) for k in range(8)]
    departures = []
    for number, (first, end) in enumerate(zip(PACK_GROUPS, PACK_GROUPS[1:])):
        arrivals[number].wait()
        for tile in range(first, end):
            block = jnp.concatenate([fields[8 * tile + k] for k in order], axis=0)
            packed[:, tile] = block.T.reshape(GROUPS, NEAR, 128)
        departures.append(
            pltpu.make_async_copy(
                packed.at[:, pl.ds(first, end - first)],
                out_ref.at[:, pl.ds(first, end - first)],
                out_sems.at[number],
            )
        )
        departures[-1].start()
    for departure in departures:
        departure.wait()


def derive_line(values, odd_table, even_table, centre):
    sums = [values[k] + values[6 - k] for k in range(3)]
    differences = [values[k] - values[6 - k] for k in range(3)]
    even = [
        sum(float(odd_table[i, j]) * differences[j] for j in range(1, 3))
        + float(odd_table[i, 0]) * differences[0]
        for i in range(4)
    ]
    odd = [
        (float(even_table[i, 0]) * sums[0] + float(even_table[i, 1]) * sums[1])
        + (float(even_table[i, 2]) * sums[2] + float(centre[i]) * values[3])
        for i in range(3)
    ]
    return (
        [even[i] + odd[i] for i in range(3)]
        + [even[3]]
        + [even[i] - odd[i] for i in (2, 1, 0)]
    )


CHUNKS = (0, 7, 13, 19, 25, 31, FIELD_TILES)
BACK_CHUNKS = (0, 5, 10, 15, BACK_TILES)


def main_kernel(
    in_ref, metric_ref, synth_ref, back_ref, jump_ref, out_ref, plane, first, second, product, *parts
):
    masks = block_masks()
    matrix = lobatto_matrix(POINTS - 1)
    mirrored = matrix[:, ::-1]
    odd_table = (matrix - mirrored)[:4, :3] / 2.0
    even_table = (matrix + mirrored)[:3, :3] / 2.0
    centre = matrix[:3, 3]

    def gather(chunk):
        for place, tile in enumerate(range(CHUNKS[chunk], CHUNKS[chunk + 1])):
            rows = slice(64 * place, 64 * place + 64)
            for half in range(2):
                swapped = gather_blocks([in_ref[8 * half + k, tile] for k in range(8)], masks)
                upper, lower = split_two(jnp.concatenate(swapped, axis=0))
                parts[chunk][rows, 128 * half : 128 * half + 128] = upper
                parts[chunk][rows, MODES + 128 * half : MODES + 128 * half + 128] = lower

    def synthesize(half, chunk):
        both = parts[chunk][...]
        deep = jnp.concatenate([both, both[:, :MODES]], axis=1)
        rows = slice(64 * CHUNKS[chunk], 64 * CHUNKS[chunk + 1])
        lanes = slice(MODES * half, MODES * half + MODES)
        plane[rows, lanes] = dot(deep, synth_ref[:, lanes])

    def derive(half, field):
        source = slice(MODES * half, MODES * half + 128)
        lanes = slice(128 * half, 128 * half + 128)

        def at(point):
            row = (field * QUAD + point) * 8
            return slice(row, row + 8)

        for line in range(POINTS):
            for stride, base, target in ((1, 7 * line, first), (7, line, second)):
                values = [plane[at(base + stride * k), source] for k in range(POINTS)]
                for k, slope in enumerate(derive_line(values, odd_table, even_table, centre)):
                    target[at(base + stride * k), lanes] = slope

    def combine(half, point):
        east_first, north_first, east_second, north_second = (metric_ref[k, point] for k in range(4))
        source = slice(MODES * half, MODES * half + 128)
        span = slice(MODES * half + 128, MODES * half + MODES)
        lanes = slice(128 * half, 128 * half + 128)

        def at(field):
            return pl.ds(pl.multiple_of((field * QUAD + point) * 8, 8), 8)

        speed = [plane[at(k), source] for k in range(3)]
        base = [plane[at(3 + k), source] for k in range(3)]
        along = sum(speed[k] * first[at(3 + k), lanes] for k in range(3))
        across = sum(speed[k] * second[at(3 + k), lanes] for k in range(3))
        turned = (
            east_first * along + east_second * across,
            north_first * along + north_second * across,
            sum(speed[k] * plane[at(3 + k), span] for k in range(3)),
        )
        flow_first = base[0] * east_first + base[1] * north_first
        flow_second = base[0] * east_second + base[1] * north_second
        for k in range(3):
            carried = (
                flow_first * first[at(k), lanes]
                + flow_second * second[at(k), lanes]
                + base[2] * plane[at(k), span]
            )
            product[at(k), lanes] = turned[k] - carried

    def analyse(chunk):
        rows = slice(64 * BACK_CHUNKS[chunk], 64 * BACK_CHUNKS[chunk + 1])
        upper, lower = split_two(product[rows, :])
        return dot(jnp.concatenate([upper, lower, upper], axis=1), back_ref[...])

    def scatter(chunk, coefficient):
        for place, tile in enumerate(range(BACK_CHUNKS[chunk], BACK_CHUNKS[chunk + 1])):
            for half in range(2):
                pieces = [
                    coefficient[64 * place + 8 * k : 64 * place + 8 * k + 8, 128 * half : 128 * half + 128]
                    for k in range(8)
                ]
                for k, swapped in enumerate(scatter_blocks(pieces, masks)):
                    out_ref[8 * half + k, tile] = swapped


    product[BACK_ROWS * 8 :, :] = jnp.zeros((BACK_TILES * 64 - BACK_ROWS * 8, MODES), jnp.float32)
    gather(0)
    for chunk in range(6):
        synthesize(0, chunk)
        if chunk < 5:
            gather(chunk + 1)
        if chunk:
            derive(0, chunk - 1)
    for chunk in range(6):
        synthesize(1, chunk)
        if chunk == 0:
            derive(0, 5)
        else:
            derive(1, chunk - 1)
    derive(1, 5)

    @pl.loop(0, QUAD, unroll=4)
    def _(point):
        combine(0, point)
        combine(1, point)
    held = analyse(0)
    for chunk in range(4):
        following = analyse(chunk + 1) if chunk < 3 else None
        scatter(chunk, held)
        held = following


def traces_of(adjoint_ref):
    return jnp.concatenate(
        [
            jnp.concatenate(
                [adjoint_ref[component * QUAD + rim_point(side, step)] for side in range(4)], axis=1
            )
            for component in range(3)
            for step in range(POINTS)
        ],
        axis=0,
    )


def send_kernel(adjoint_ref, sides_ref, *out_refs):
    traces = traces_of(adjoint_ref)
    chosen = lax.broadcasted_iota(jnp.int32, (512, 4 * SLOTS), 0) == sides_ref[...]
    chosen = jnp.where(chosen, 1.0, 0.0).astype(jnp.bfloat16)
    outgoing = sum(dot(part, chosen) for part in split_three(traces))
    padding = jnp.zeros((TRACE_LANES - TRACE_ROWS, 128), jnp.float32)
    outgoing = jnp.concatenate([outgoing, padding], axis=0).T
    for direction, out_ref in enumerate(out_refs):
        out_ref[...] = outgoing[direction * SLOTS : (direction + 1) * SLOTS]


def ready_kernel(
    group_ref, metric_ref, synth_ref, back_ref, out_ref, synth_out, back_out, turned, sems
):
    copies = []
    for source, target in ((synth_ref, synth_out), (back_ref, back_out)):
        for place, part in enumerate((0, 0, 1)):
            copies.append(
                pltpu.make_async_copy(
                    source.at[pl.ds(MODES * part, MODES)],
                    target.at[pl.ds(MODES * place, MODES)],
                    sems.at[len(copies)],
                )
            )
            copies[-1].start()
    turned[...] = jnp.concatenate(
        [metric_ref[...], jnp.zeros((256 - 4 * QUAD, 128), jnp.float32)], axis=0
    ).T
    own = turned[pl.ds(pl.multiple_of(group_ref[0] * NEAR, NEAR), NEAR), :]
    for index in range(4 * QUAD):
        out_ref[index] = jnp.broadcast_to(own[:, index : index + 1], (NEAR, 128))
    for copy in copies:
        copy.wait()


def jump_kernel(adjoint_ref, index_ref, penalty_ref, *refs):
    received_refs, out_ref = refs[:4], refs[4]
    traces = traces_of(adjoint_ref)
    received = jnp.concatenate([ref[...] for ref in received_refs], axis=0).T[:TRACE_ROWS]
    index = index_ref[...]
    where_local = lax.broadcasted_iota(jnp.int32, (512, 128), 0)
    where_far = lax.broadcasted_iota(jnp.int32, (128, 128), 0) + 512
    local_parts = split_three(traces)
    far_parts = split_three(received)
    for side in range(4):
        wanted = index[side : side + 1]
        near = jnp.where(where_local == wanted, 1.0, 0.0).astype(jnp.bfloat16)
        far = jnp.where(where_far == wanted, 1.0, 0.0).astype(jnp.bfloat16)
        outer = sum(dot(part, near) for part in local_parts) + sum(
            dot(part, far) for part in far_parts
        )
        for component in range(3):
            for step in range(POINTS):
                row = (component * POINTS + step) * GROUPS
                far_row = (component * POINTS + 6 - step) * GROUPS
                weight = penalty_ref[side * POINTS + step : side * POINTS + step + 1]
                inner = adjoint_ref[component * QUAD + rim_point(side, step)]
                jump = outer[far_row : far_row + GROUPS] - inner
                out_ref[(component * POINTS + step) * 4 + side] = weight * jump


BACK_GROUPS = (0, 7, 13, BACK_TILES)


def unpack_kernel(group_ref, in_ref, jump_ref, out_ref, advect, sems):
    turn = group_ref[0] % 8
    sides_at = {}
    for side in range(4):
        for step in range(POINTS):
            sides_at.setdefault(rim_point(side, step), []).append((side, step))
    departures = []
    for component in range(3):
        for tile in range(BACK_GROUPS[component], BACK_GROUPS[component + 1]):
            block = in_ref[:, tile].reshape(128, 128).T
            for k in range(8):
                row = 8 * tile + lax.rem(k - turn + 8, 8)
                advect[row] = block[16 * k : 16 * k + 16]
        first = component * QUAD
        for point, sides in sides_at.items():
            value = advect[first + point]
            for side, step in sides:
                value = value + jump_ref[(component * POINTS + step) * 4 + side]
            advect[first + point] = value
        departures.append(
            pltpu.make_async_copy(
                advect.at[pl.ds(first, QUAD)], out_ref.at[pl.ds(first, QUAD)], sems.at[component]
            )
        )
        departures[-1].start()
    for departure in departures:
        departure.wait()


def call(kernel, outs, *args, places=None, scratch=(), grant=12):
    spaces = {"v": pltpu.VMEM, "h": pltpu.HBM, "s": pltpu.SMEM, "a": pl.ANY}
    places = places or "v" * len(args)
    many = isinstance(outs, list)
    outs = [
        jax.ShapeDtypeStruct(o, jnp.float32) if isinstance(o, tuple) else o
        for o in (outs if many else [outs])
    ]
    out_specs = [
        pl.BlockSpec(memory_space=getattr(o, "memory_space", None) or pltpu.VMEM) for o in outs
    ]
    moved = sum(int(np.prod(a.shape)) * a.dtype.itemsize for a in (*args, *outs))
    args = [
        pltpu.with_memory_space_constraint(a, pltpu.HBM) if p == "h" else a
        for a, p in zip(args, places)
    ]
    return pl.pallas_call(
        kernel,
        out_shape=outs if many else outs[0],
        in_specs=[pl.BlockSpec(memory_space=spaces[p]) for p in places],
        out_specs=out_specs if many else out_specs[0],
        scratch_shapes=list(scratch),
        compiler_params=pltpu.CompilerParams(vmem_limit_bytes=grant * MEBI),
        cost_estimate=pl.CostEstimate(flops=0, bytes_accessed=moved, transcendentals=0),
    )(*args)


def passed_along(block, axis, distance):
    count = lax.axis_size(axis)
    return lax.ppermute(block, axis, [((i - distance) % count, i) for i in range(count)])


def shards(adjoint, base_flow, metric, penalty, send_sides, ext_index):
    synthesis, analysis, slope = fourier_tables()
    by_half = np.arange(2 * MODES).reshape(2, 2, 128).transpose(1, 0, 2).reshape(-1)
    synth = stacked(np.concatenate([synthesis, slope], axis=0)[by_half].T)
    back = stacked(analysis.T)
    natural = jnp.transpose(adjoint, (0, 2, 1, 3)).reshape(BACK_ROWS, GROUPS, 128)
    base = jnp.transpose(base_flow, (0, 2, 1, 3)).reshape(BACK_ROWS, GROUPS, 128)
    group = lax.axis_index("mode").reshape(1)

    packed = call(
        pack_kernel,
        pltpu.HBM((GROUPS, FIELD_TILES, NEAR, 128), jnp.float32),
        group,
        natural,
        base,
        places="shh",
        scratch=[
            pltpu.VMEM((8 * FIELD_TILES, GROUPS, 128), jnp.float32),
            pltpu.VMEM((GROUPS, FIELD_TILES, NEAR, 128), jnp.float32),
            pltpu.SemaphoreType.DMA((6,)),
            pltpu.SemaphoreType.DMA((6,)),
        ],
    )
    arrived = lax.all_to_all(packed, "mode", split_axis=0, concat_axis=0, tiled=True)

    outgoing = call(
        send_kernel, [(SLOTS, TRACE_LANES)] * 4, natural, send_sides.reshape(1, 4 * SLOTS)
    )
    received = [passed_along(block, "elem", o) for block, o in zip(outgoing, OFFSETS)]
    own_metric, synth, back = call(
        ready_kernel,
        [
            pltpu.VMEM((4 * QUAD, NEAR, 128), jnp.float32),
            pltpu.VMEM((3 * MODES, 2 * MODES), jnp.bfloat16),
            pltpu.VMEM((3 * MODES, MODES), jnp.bfloat16),
        ],
        group,
        metric.reshape(4 * QUAD, 128),
        jnp.asarray(synth),
        jnp.asarray(back),
        places="svhh",
        scratch=[pltpu.VMEM((128, 256), jnp.float32), pltpu.SemaphoreType.DMA((6,))],
    )
    jumps = call(
        jump_kernel,
        (84, GROUPS, 128),
        natural,
        ext_index,
        penalty.reshape(4 * POINTS, 128),
        *received,
    )

    coefficients = call(
        main_kernel,
        (GROUPS, BACK_TILES, NEAR, 128),
        arrived,
        own_metric.reshape(4, QUAD, NEAR, 128),
        synth,
        back,
        jumps,
        places="vvvva",
        scratch=[
            pltpu.VMEM((64 * FIELD_TILES, 2 * MODES), jnp.float32),
            pltpu.VMEM((8 * ROWS, MODES), jnp.float32),
            pltpu.VMEM((8 * ROWS, MODES), jnp.float32),
            pltpu.VMEM((64 * BACK_TILES, MODES), jnp.float32),
        ]
        + [
            pltpu.VMEM((64 * (end - first), 2 * MODES), jnp.bfloat16)
            for first, end in zip(CHUNKS, CHUNKS[1:])
        ],
        grant=28,
    )
    returned = lax.all_to_all(coefficients, "mode", split_axis=0, concat_axis=0, tiled=True)
    out = call(
        unpack_kernel,
        pltpu.HBM((BACK_ROWS, GROUPS, 128), jnp.float32),
        group,
        returned,
        jumps,
        places="svv",
        scratch=[
            pltpu.VMEM((8 * BACK_TILES, GROUPS, 128), jnp.float32),
            pltpu.SemaphoreType.DMA((3,)),
        ],
    )
    return jnp.transpose(out.reshape(3, QUAD, GROUPS, 128), (0, 2, 1, 3))


def solution(mesh):
    placed = (
        P(None, "mode", None, "elem"),
        P(None, "mode", None, "elem"),
        P(None, None, "elem"),
        P(None, None, "elem"),
        P("elem", None, None),
        P(None, "elem"),
    )
    return jax.shard_map(
        shards, mesh=mesh, in_specs=placed, out_specs=P(None, "mode", None, "elem"), check_vma=False
    )
```

```python
import math

import jax
import jax.numpy as jnp
import numpy as np
from jax import lax
from jax.experimental import pallas as pl
from jax.experimental.pallas import tpu as pltpu
from jax.sharding import PartitionSpec as P

MODES = 256
POINTS = 7
QUAD = 49
GROUPS = 16
NEAR = 8
ROWS = 6 * QUAD
FIELD_TILES = 37
BACK_ROWS = 3 * QUAD
BACK_TILES = 19
SLOTS = 32
OFFSETS = (1, -1, 2, -2)
TRACE_ROWS = 3 * POINTS * GROUPS
TRACE_LANES = 384
MEBI = 1024 * 1024


def legendre_pair(degree, position):
    previous = 1.0
    current = position
    for order_index in range(2, degree + 1):
        following = (
            (2 * order_index - 1) * position * current - (order_index - 1) * previous
        ) / order_index
        previous = current
        current = following
    return (current, previous)


def lobatto_points(degree):
    node_list = []
    for point_index in range(degree + 1):
        estimate = -math.cos(math.pi * point_index / degree)
        for newton_step in range(60):
            current, previous = legendre_pair(degree, estimate)
            estimate = estimate - (estimate * current - previous) / ((degree + 1) * current)
        node_list.append(estimate)
    node_list[0] = -1.0
    node_list[degree] = 1.0
    return node_list


def lobatto_matrix(degree):
    nodes = lobatto_points(degree)
    at_nodes = [legendre_pair(degree, value)[0] for value in nodes]
    count = degree + 1
    matrix = np.zeros((count, count))
    for row in range(count):
        for col in range(count):
            if row != col:
                matrix[row, col] = at_nodes[row] / (at_nodes[col] * (nodes[row] - nodes[col]))
    matrix[0, 0] = -degree * (degree + 1) / 4.0
    matrix[degree, degree] = degree * (degree + 1) / 4.0
    return matrix


def fourier_tables():
    planes = np.arange(MODES)[:, None]
    slot = np.arange(MODES)[None, :]
    wavenumber = slot // 2
    angles = (wavenumber * planes % MODES) * (2.0 * math.pi / MODES)
    synthesis = np.where(slot % 2 == 1, -np.sin(angles), np.cos(angles))
    synthesis = np.where(slot == 1, np.where(planes % 2 == 0, 1.0, -1.0), synthesis)
    weights = np.where(slot < 2, 1.0, 2.0) / MODES
    analysis = (synthesis * weights).T
    rates = wavenumber * (4.0 / MODES)
    slope = np.zeros((MODES, MODES))
    slope[:, 0::2] = rates[:, 0::2] * synthesis[:, 1::2]
    slope[:, 1::2] = -rates[:, 0::2] * synthesis[:, 0::2]
    return synthesis, analysis, slope


def stacked(table):
    table = table.astype(np.float32)
    high = table.astype(jnp.bfloat16)
    low = (table - high.astype(np.float32)).astype(jnp.bfloat16)
    return np.concatenate([high, low], axis=0)


def rim_point(side, step):
    last = POINTS - 1
    return (step, POINTS * step + last, POINTS * last + last - step, POINTS * (last - step))[side]


def barrel(turned, masks):
    moved = [turned[-k % 8] for k in range(8)]
    for bit in range(3):
        moved = [jnp.where(masks[bit], moved[(k - (1 << bit)) % 8], moved[k]) for k in range(8)]
    return moved


def gather_blocks(turned, masks):
    return [
        pltpu.roll(tile, 128 - 16 * g, 1) if g else tile
        for g, tile in enumerate(barrel(turned, masks))
    ]


def scatter_blocks(tiles, masks):
    return barrel([pltpu.roll(tile, 16 * q, 1) if q else tile for q, tile in enumerate(tiles)], masks)


def block_masks():
    block = lax.broadcasted_iota(jnp.int32, (8, 128), 1) // 16
    return [(block & (1 << bit)) != 0 for bit in range(3)]


def split_two(value):
    high = value.astype(jnp.bfloat16)
    low = (value - high.astype(jnp.float32)).astype(jnp.bfloat16)
    return high, low


def split_three(value):
    high = value.astype(jnp.bfloat16)
    rest = value - high.astype(jnp.float32)
    middle = rest.astype(jnp.bfloat16)
    low = (rest - middle.astype(jnp.float32)).astype(jnp.bfloat16)
    return high, middle, low


def dot(left, right):
    return jnp.dot(left, right, preferred_element_type=jnp.float32)


ADJOINT_CUTS = (0, 48, 96, BACK_ROWS)
BASE_CUTS = (0, 48, 96, 128, BACK_ROWS)
PACK_GROUPS = (0, 6, 12, 18, 24, 30, 34, FIELD_TILES)


def pack_kernel(group_ref, adjoint_ref, base_ref, out_ref, fields, packed, in_sems, out_sems):
    arrivals = []
    sources = ((adjoint_ref, 0, ADJOINT_CUTS), (base_ref, BACK_ROWS, BASE_CUTS))
    for source, offset, cuts in sources:
        for first, end in zip(cuts, cuts[1:]):
            arrivals.append(
                pltpu.make_async_copy(
                    source.at[pl.ds(first, end - first)],
                    fields.at[pl.ds(offset + first, end - first)],
                    in_sems.at[len(arrivals)],
                )
            )
            arrivals[-1].start()
    fields[ROWS:] = jnp.zeros((8 * FIELD_TILES - ROWS, GROUPS, 128), jnp.float32)
    turn = group_ref[0] % 8
    order = [lax.rem(k - turn + 8, 8) for k in range(8)]
    departures = []
    for number, (first, end) in enumerate(zip(PACK_GROUPS, PACK_GROUPS[1:])):
        arrivals[number].wait()
        for tile in range(first, end):
            block = jnp.concatenate([fields[8 * tile + k] for k in order], axis=0)
            packed[:, tile] = block.T.reshape(GROUPS, NEAR, 128)
        departures.append(
            pltpu.make_async_copy(
                packed.at[:, pl.ds(first, end - first)],
                out_ref.at[:, pl.ds(first, end - first)],
                out_sems.at[number],
            )
        )
        departures[-1].start()
    for departure in departures:
        departure.wait()


def derive_line(values, odd_table, even_table, centre):
    sums = [values[k] + values[6 - k] for k in range(3)]
    differences = [values[k] - values[6 - k] for k in range(3)]
    even = [
        sum(float(odd_table[i, j]) * differences[j] for j in range(1, 3))
        + float(odd_table[i, 0]) * differences[0]
        for i in range(4)
    ]
    odd = [
        (float(even_table[i, 0]) * sums[0] + float(even_table[i, 1]) * sums[1])
        + (float(even_table[i, 2]) * sums[2] + float(centre[i]) * values[3])
        for i in range(3)
    ]
    return (
        [even[i] + odd[i] for i in range(3)]
        + [even[3]]
        + [even[i] - odd[i] for i in (2, 1, 0)]
    )


CHUNKS = (0, 7, 13, 19, 25, 31, FIELD_TILES)
BACK_CHUNKS = (0, 5, 10, 15, BACK_TILES)


def main_kernel(
    in_ref,
    metric_hbm,
    synth_ref,
    back_hbm,
    jump_ref,
    out_ref,
    metric_ref,
    back_ref,
    sems,
    plane,
    first,
    second,
    product,
    *parts,
):
    metric_copy = pltpu.make_async_copy(metric_hbm, metric_ref, sems.at[3])
    metric_copy.start()
    back_copies = stack_table(back_hbm, back_ref, sems)
    masks = block_masks()
    matrix = lobatto_matrix(POINTS - 1)
    mirrored = matrix[:, ::-1]
    odd_table = (matrix - mirrored)[:4, :3] / 2.0
    even_table = (matrix + mirrored)[:3, :3] / 2.0
    centre = matrix[:3, 3]

    def gather(chunk):
        for place, tile in enumerate(range(CHUNKS[chunk], CHUNKS[chunk + 1])):
            rows = slice(64 * place, 64 * place + 64)
            for half in range(2):
                swapped = gather_blocks([in_ref[8 * half + k, tile] for k in range(8)], masks)
                upper, lower = split_two(jnp.concatenate(swapped, axis=0))
                parts[chunk][rows, 128 * half : 128 * half + 128] = upper
                parts[chunk][rows, MODES + 128 * half : MODES + 128 * half + 128] = lower

    def synthesize(half, chunk):
        both = parts[chunk][...]
        deep = jnp.concatenate([both, both[:, :MODES]], axis=1)
        rows = slice(64 * CHUNKS[chunk], 64 * CHUNKS[chunk + 1])
        lanes = slice(MODES * half, MODES * half + MODES)
        plane[rows, lanes] = dot(deep, synth_ref[:, lanes])

    def derive(half, field):
        source = slice(MODES * half, MODES * half + 128)
        lanes = slice(128 * half, 128 * half + 128)

        def at(point):
            row = (field * QUAD + point) * 8
            return slice(row, row + 8)

        for line in range(POINTS):
            for stride, base, target in ((1, 7 * line, first), (7, line, second)):
                values = [plane[at(base + stride * k), source] for k in range(POINTS)]
                for k, slope in enumerate(derive_line(values, odd_table, even_table, centre)):
                    target[at(base + stride * k), lanes] = slope

    def combine(half, point):
        east_first, north_first, east_second, north_second = (
            metric_ref[k * QUAD + point] for k in range(4)
        )
        source = slice(MODES * half, MODES * half + 128)
        span = slice(MODES * half + 128, MODES * half + MODES)
        lanes = slice(128 * half, 128 * half + 128)

        def at(field):
            return pl.ds(pl.multiple_of((field * QUAD + point) * 8, 8), 8)

        speed = [plane[at(k), source] for k in range(3)]
        base = [plane[at(3 + k), source] for k in range(3)]
        along = sum(speed[k] * first[at(3 + k), lanes] for k in range(3))
        across = sum(speed[k] * second[at(3 + k), lanes] for k in range(3))
        turned = (
            east_first * along + east_second * across,
            north_first * along + north_second * across,
            sum(speed[k] * plane[at(3 + k), span] for k in range(3)),
        )
        flow_first = base[0] * east_first + base[1] * north_first
        flow_second = base[0] * east_second + base[1] * north_second
        for k in range(3):
            carried = (
                flow_first * first[at(k), lanes]
                + flow_second * second[at(k), lanes]
                + base[2] * plane[at(k), span]
            )
            product[at(k), lanes] = turned[k] - carried

    def analyse(chunk):
        rows = slice(64 * BACK_CHUNKS[chunk], 64 * BACK_CHUNKS[chunk + 1])
        upper, lower = split_two(product[rows, :])
        return dot(jnp.concatenate([upper, lower, upper], axis=1), back_ref[...])

    def scatter(chunk, coefficient):
        for place, tile in enumerate(range(BACK_CHUNKS[chunk], BACK_CHUNKS[chunk + 1])):
            for half in range(2):
                pieces = [
                    coefficient[64 * place + 8 * k : 64 * place + 8 * k + 8, 128 * half : 128 * half + 128]
                    for k in range(8)
                ]
                for k, swapped in enumerate(scatter_blocks(pieces, masks)):
                    out_ref[8 * half + k, tile] = swapped


    product[BACK_ROWS * 8 :, :] = jnp.zeros((BACK_TILES * 64 - BACK_ROWS * 8, MODES), jnp.float32)
    gather(0)
    for chunk in range(6):
        synthesize(0, chunk)
        if chunk < 5:
            gather(chunk + 1)
        if chunk:
            derive(0, chunk - 1)
    for chunk in range(6):
        synthesize(1, chunk)
        if chunk == 0:
            derive(0, 5)
        else:
            derive(1, chunk - 1)
    derive(1, 5)
    metric_copy.wait()
    for copy in back_copies:
        copy.wait()

    @pl.loop(0, QUAD, unroll=4)
    def _(point):
        combine(0, point)
        combine(1, point)
    held = analyse(0)
    for chunk in range(4):
        following = analyse(chunk + 1) if chunk < 3 else None
        scatter(chunk, held)
        held = following


def traces_of(adjoint_ref):
    return jnp.concatenate(
        [
            jnp.concatenate(
                [adjoint_ref[component * QUAD + rim_point(side, step)] for side in range(4)], axis=1
            )
            for component in range(3)
            for step in range(POINTS)
        ],
        axis=0,
    )


def fetch(source, target, sem):
    copy = pltpu.make_async_copy(source, target, sem)
    copy.start()
    copy.wait()


def send_kernel(adjoint_hbm, sides_ref, *refs):
    out_refs, (adjoint_ref, sem) = refs[:4], refs[4:]
    fetch(adjoint_hbm, adjoint_ref, sem)
    traces = traces_of(adjoint_ref)
    chosen = lax.broadcasted_iota(jnp.int32, (512, 4 * SLOTS), 0) == sides_ref[...]
    chosen = jnp.where(chosen, 1.0, 0.0).astype(jnp.bfloat16)
    outgoing = sum(dot(part, chosen) for part in split_three(traces))
    padding = jnp.zeros((TRACE_LANES - TRACE_ROWS, 128), jnp.float32)
    outgoing = jnp.concatenate([outgoing, padding], axis=0).T
    for direction, out_ref in enumerate(out_refs):
        out_ref[...] = outgoing[direction * SLOTS : (direction + 1) * SLOTS]


def stack_table(source, target, sems):
    copies = [
        pltpu.make_async_copy(
            source.at[pl.ds(MODES * part, MODES)],
            target.at[pl.ds(MODES * place, MODES)],
            sems.at[place],
        )
        for place, part in enumerate((0, 0, 1))
    ]
    for copy in copies:
        copy.start()
    return copies


def ready_kernel(group_ref, metric_ref, synth_ref, out_ref, synth_out, turned, spread, sems):
    copies = stack_table(synth_ref, synth_out, sems)
    turned[...] = jnp.concatenate(
        [metric_ref[...], jnp.zeros((256 - 4 * QUAD, 128), jnp.float32)], axis=0
    ).T
    own = turned[pl.ds(pl.multiple_of(group_ref[0] * NEAR, NEAR), NEAR), :]
    for index in range(4 * QUAD):
        spread[index] = jnp.broadcast_to(own[:, index : index + 1], (NEAR, 128))
    copies.append(pltpu.make_async_copy(spread, out_ref, sems.at[3]))
    copies[-1].start()
    for copy in copies:
        copy.wait()


def jump_kernel(adjoint_hbm, index_ref, penalty_ref, *refs):
    received_refs, (out_ref, adjoint_ref, held, sem) = refs[:4], refs[4:]
    fetch(adjoint_hbm, adjoint_ref, sem)
    traces = traces_of(adjoint_ref)
    received = jnp.concatenate([ref[...] for ref in received_refs], axis=0).T[:TRACE_ROWS]
    index = index_ref[...]
    where_local = lax.broadcasted_iota(jnp.int32, (512, 128), 0)
    where_far = lax.broadcasted_iota(jnp.int32, (128, 128), 0) + 512
    local_parts = split_three(traces)
    far_parts = split_three(received)
    for side in range(4):
        wanted = index[side : side + 1]
        near = jnp.where(where_local == wanted, 1.0, 0.0).astype(jnp.bfloat16)
        far = jnp.where(where_far == wanted, 1.0, 0.0).astype(jnp.bfloat16)
        outer = sum(dot(part, near) for part in local_parts) + sum(
            dot(part, far) for part in far_parts
        )
        for component in range(3):
            for step in range(POINTS):
                row = (component * POINTS + step) * GROUPS
                far_row = (component * POINTS + 6 - step) * GROUPS
                weight = penalty_ref[side * POINTS + step : side * POINTS + step + 1]
                inner = adjoint_ref[component * QUAD + rim_point(side, step)]
                jump = outer[far_row : far_row + GROUPS] - inner
                held[(component * POINTS + step) * 4 + side] = weight * jump
    fetch(held, out_ref, sem)


BACK_GROUPS = (0, 7, 13, BACK_TILES)


def unpack_kernel(group_ref, in_ref, jump_hbm, out_ref, advect, jump_ref, sems):
    arrivals = [
        pltpu.make_async_copy(
            jump_hbm.at[pl.ds(28 * component, 28)],
            jump_ref.at[pl.ds(28 * component, 28)],
            sems.at[3 + component],
        )
        for component in range(3)
    ]
    for arrival in arrivals:
        arrival.start()
    turn = group_ref[0] % 8
    sides_at = {}
    for side in range(4):
        for step in range(POINTS):
            sides_at.setdefault(rim_point(side, step), []).append((side, step))
    departures = []
    for component in range(3):
        for tile in range(BACK_GROUPS[component], BACK_GROUPS[component + 1]):
            block = in_ref[:, tile].reshape(128, 128).T
            for k in range(8):
                row = 8 * tile + lax.rem(k - turn + 8, 8)
                advect[row] = block[16 * k : 16 * k + 16]
        first = component * QUAD
        arrivals[component].wait()
        for point, sides in sides_at.items():
            value = advect[first + point]
            for side, step in sides:
                value = value + jump_ref[(component * POINTS + step) * 4 + side]
            advect[first + point] = value
        departures.append(
            pltpu.make_async_copy(
                advect.at[pl.ds(first, QUAD)], out_ref.at[pl.ds(first, QUAD)], sems.at[component]
            )
        )
        departures[-1].start()
    for departure in departures:
        departure.wait()


def call(kernel, outs, *args, places=None, scratch=(), grant=12):
    spaces = {"v": pltpu.VMEM, "V": pltpu.VMEM, "h": pltpu.HBM, "s": pltpu.SMEM}
    places = places or "v" * len(args)
    many = isinstance(outs, list)
    outs = [
        jax.ShapeDtypeStruct(o, jnp.float32) if isinstance(o, tuple) else o
        for o in (outs if many else [outs])
    ]
    out_specs = [
        pl.BlockSpec(memory_space=getattr(o, "memory_space", None) or pltpu.VMEM) for o in outs
    ]
    moved = sum(int(np.prod(a.shape)) * a.dtype.itemsize for a in (*args, *outs))
    args = [
        pltpu.with_memory_space_constraint(a, spaces[p]) if p in "hV" else a
        for a, p in zip(args, places)
    ]
    return pl.pallas_call(
        kernel,
        out_shape=outs if many else outs[0],
        in_specs=[pl.BlockSpec(memory_space=spaces[p]) for p in places],
        out_specs=out_specs if many else out_specs[0],
        scratch_shapes=list(scratch),
        compiler_params=pltpu.CompilerParams(vmem_limit_bytes=grant * MEBI),
        cost_estimate=pl.CostEstimate(flops=0, bytes_accessed=moved, transcendentals=0),
    )(*args)


def passed_along(block, axis, distance):
    count = lax.axis_size(axis)
    return lax.ppermute(block, axis, [((i - distance) % count, i) for i in range(count)])


def shards(adjoint, base_flow, metric, penalty, send_sides, ext_index):
    synthesis, analysis, slope = fourier_tables()
    by_half = np.arange(2 * MODES).reshape(2, 2, 128).transpose(1, 0, 2).reshape(-1)
    synth = stacked(np.concatenate([synthesis, slope], axis=0)[by_half].T)
    back = stacked(analysis.T)
    natural = jnp.transpose(adjoint, (0, 2, 1, 3)).reshape(BACK_ROWS, GROUPS, 128)
    base = jnp.transpose(base_flow, (0, 2, 1, 3)).reshape(BACK_ROWS, GROUPS, 128)
    group = lax.axis_index("mode").reshape(1)

    packed = call(
        pack_kernel,
        pltpu.HBM((GROUPS, FIELD_TILES, NEAR, 128), jnp.float32),
        group,
        natural,
        base,
        places="shh",
        scratch=[
            pltpu.VMEM((8 * FIELD_TILES, GROUPS, 128), jnp.float32),
            pltpu.VMEM((GROUPS, FIELD_TILES, NEAR, 128), jnp.float32),
            pltpu.SemaphoreType.DMA((7,)),
            pltpu.SemaphoreType.DMA((7,)),
        ],
    )
    arrived = lax.all_to_all(packed, "mode", split_axis=0, concat_axis=0, tiled=True)

    outgoing = call(
        send_kernel,
        [(SLOTS, TRACE_LANES)] * 4,
        natural,
        send_sides.reshape(1, 4 * SLOTS),
        places="hv",
        scratch=[
            pltpu.VMEM((BACK_ROWS, GROUPS, 128), jnp.float32),
            pltpu.SemaphoreType.DMA(()),
        ],
    )
    received = [passed_along(block, "elem", o) for block, o in zip(outgoing, OFFSETS)]
    own_metric, synth = call(
        ready_kernel,
        [
            pltpu.HBM((4 * QUAD, NEAR, 128), jnp.float32),
            pltpu.VMEM((3 * MODES, 2 * MODES), jnp.bfloat16),
        ],
        group,
        metric.reshape(4 * QUAD, 128),
        jnp.asarray(synth),
        places="svh",
        scratch=[
            pltpu.VMEM((128, 256), jnp.float32),
            pltpu.VMEM((4 * QUAD, NEAR, 128), jnp.float32),
            pltpu.SemaphoreType.DMA((4,)),
        ],
    )
    jumps = call(
        jump_kernel,
        pltpu.HBM((84, GROUPS, 128), jnp.float32),
        natural,
        ext_index,
        penalty.reshape(4 * POINTS, 128),
        *received,
        places="hvvvvvv",
        scratch=[
            pltpu.VMEM((BACK_ROWS, GROUPS, 128), jnp.float32),
            pltpu.VMEM((84, GROUPS, 128), jnp.float32),
            pltpu.SemaphoreType.DMA(()),
        ],
    )

    coefficients = call(
        main_kernel,
        (GROUPS, BACK_TILES, NEAR, 128),
        arrived,
        own_metric,
        synth,
        jnp.asarray(back),
        jumps,
        places="Vhvhh",
        scratch=[
            pltpu.VMEM((4 * QUAD, NEAR, 128), jnp.float32),
            pltpu.VMEM((3 * MODES, MODES), jnp.bfloat16),
            pltpu.SemaphoreType.DMA((4,)),
            pltpu.VMEM((64 * FIELD_TILES, 2 * MODES), jnp.float32),
            pltpu.VMEM((8 * ROWS, MODES), jnp.float32),
            pltpu.VMEM((8 * ROWS, MODES), jnp.float32),
            pltpu.VMEM((64 * BACK_TILES, MODES), jnp.float32),
        ]
        + [
            pltpu.VMEM((64 * (end - first), 2 * MODES), jnp.bfloat16)
            for first, end in zip(CHUNKS, CHUNKS[1:])
        ],
        grant=28,
    )
    returned = lax.all_to_all(coefficients, "mode", split_axis=0, concat_axis=0, tiled=True)
    out = call(
        unpack_kernel,
        pltpu.HBM((BACK_ROWS, GROUPS, 128), jnp.float32),
        group,
        returned,
        jumps,
        places="svh",
        scratch=[
            pltpu.VMEM((8 * BACK_TILES, GROUPS, 128), jnp.float32),
            pltpu.VMEM((84, GROUPS, 128), jnp.float32),
            pltpu.SemaphoreType.DMA((6,)),
        ],
    )
    return jnp.transpose(out.reshape(3, QUAD, GROUPS, 128), (0, 2, 1, 3))


def solution(mesh):
    placed = (
        P(None, "mode", None, "elem"),
        P(None, "mode", None, "elem"),
        P(None, None, "elem"),
        P(None, None, "elem"),
        P("elem", None, None),
        P(None, "elem"),
    )
    return jax.shard_map(
        shards, mesh=mesh, in_specs=placed, out_specs=P(None, "mode", None, "elem"), check_vma=False
    )
```

```python
import math

import jax
import jax.numpy as jnp
import numpy as np
from jax import lax
from jax.experimental import pallas as pl
from jax.experimental.pallas import tpu as pltpu
from jax.sharding import PartitionSpec as P

MODES = 256
POINTS = 7
QUAD = 49
GROUPS = 16
NEAR = 8
ROWS = 6 * QUAD
FIELD_TILES = 37
BACK_ROWS = 3 * QUAD
BACK_TILES = 19
SLOTS = 32
OFFSETS = (1, -1, 2, -2)
TRACE_ROWS = 3 * POINTS * GROUPS
TRACE_LANES = 384
MEBI = 1024 * 1024


def legendre_pair(degree, position):
    previous = 1.0
    current = position
    for order_index in range(2, degree + 1):
        following = (
            (2 * order_index - 1) * position * current - (order_index - 1) * previous
        ) / order_index
        previous = current
        current = following
    return (current, previous)


def lobatto_points(degree):
    node_list = []
    for point_index in range(degree + 1):
        estimate = -math.cos(math.pi * point_index / degree)
        for newton_step in range(60):
            current, previous = legendre_pair(degree, estimate)
            estimate = estimate - (estimate * current - previous) / ((degree + 1) * current)
        node_list.append(estimate)
    node_list[0] = -1.0
    node_list[degree] = 1.0
    return node_list


def lobatto_matrix(degree):
    nodes = lobatto_points(degree)
    at_nodes = [legendre_pair(degree, value)[0] for value in nodes]
    count = degree + 1
    matrix = np.zeros((count, count))
    for row in range(count):
        for col in range(count):
            if row != col:
                matrix[row, col] = at_nodes[row] / (at_nodes[col] * (nodes[row] - nodes[col]))
    matrix[0, 0] = -degree * (degree + 1) / 4.0
    matrix[degree, degree] = degree * (degree + 1) / 4.0
    return matrix


def fourier_tables():
    planes = np.arange(MODES)[:, None]
    slot = np.arange(MODES)[None, :]
    wavenumber = slot // 2
    angles = (wavenumber * planes % MODES) * (2.0 * math.pi / MODES)
    synthesis = np.where(slot % 2 == 1, -np.sin(angles), np.cos(angles))
    synthesis = np.where(slot == 1, np.where(planes % 2 == 0, 1.0, -1.0), synthesis)
    weights = np.where(slot < 2, 1.0, 2.0) / MODES
    analysis = (synthesis * weights).T
    rates = wavenumber * (4.0 / MODES)
    slope = np.zeros((MODES, MODES))
    slope[:, 0::2] = rates[:, 0::2] * synthesis[:, 1::2]
    slope[:, 1::2] = -rates[:, 0::2] * synthesis[:, 0::2]
    return synthesis, analysis, slope


def stacked(table):
    table = table.astype(np.float32)
    high = table.astype(jnp.bfloat16)
    low = (table - high.astype(np.float32)).astype(jnp.bfloat16)
    return np.concatenate([high, low], axis=0)


def rim_point(side, step):
    last = POINTS - 1
    return (step, POINTS * step + last, POINTS * last + last - step, POINTS * (last - step))[side]


def barrel(turned, masks):
    moved = [turned[-k % 8] for k in range(8)]
    for bit in range(3):
        moved = [jnp.where(masks[bit], moved[(k - (1 << bit)) % 8], moved[k]) for k in range(8)]
    return moved


def gather_blocks(turned, masks):
    return [
        pltpu.roll(tile, 128 - 16 * g, 1) if g else tile
        for g, tile in enumerate(barrel(turned, masks))
    ]


def scatter_blocks(tiles, masks):
    return barrel([pltpu.roll(tile, 16 * q, 1) if q else tile for q, tile in enumerate(tiles)], masks)


def block_masks():
    block = lax.broadcasted_iota(jnp.int32, (8, 128), 1) // 16
    return [(block & (1 << bit)) != 0 for bit in range(3)]


def split_two(value):
    high = value.astype(jnp.bfloat16)
    low = (value - high.astype(jnp.float32)).astype(jnp.bfloat16)
    return high, low


def split_three(value):
    high = value.astype(jnp.bfloat16)
    rest = value - high.astype(jnp.float32)
    middle = rest.astype(jnp.bfloat16)
    low = (rest - middle.astype(jnp.float32)).astype(jnp.bfloat16)
    return high, middle, low


def dot(left, right):
    return jnp.dot(left, right, preferred_element_type=jnp.float32)


ADJOINT_CUTS = (0, 48, 96, BACK_ROWS)
BASE_CUTS = (0, 48, 96, 128, BACK_ROWS)
PACK_GROUPS = (0, 6, 12, 18, 24, 30, 34, FIELD_TILES)


def pack_kernel(group_ref, adjoint_ref, base_ref, out_ref, fields, packed, in_sems, out_sems):
    arrivals = []
    sources = ((adjoint_ref, 0, ADJOINT_CUTS), (base_ref, BACK_ROWS, BASE_CUTS))
    for source, offset, cuts in sources:
        for first, end in zip(cuts, cuts[1:]):
            arrivals.append(
                pltpu.make_async_copy(
                    source.at[pl.ds(first, end - first)],
                    fields.at[pl.ds(offset + first, end - first)],
                    in_sems.at[len(arrivals)],
                )
            )
            arrivals[-1].start()
    fields[ROWS:] = jnp.zeros((8 * FIELD_TILES - ROWS, GROUPS, 128), jnp.float32)
    turn = group_ref[0] % 8
    order = [lax.rem(k - turn + 8, 8) for k in range(8)]
    departures = []
    for number, (first, end) in enumerate(zip(PACK_GROUPS, PACK_GROUPS[1:])):
        arrivals[number].wait()
        for tile in range(first, end):
            block = jnp.concatenate([fields[8 * tile + k] for k in order], axis=0)
            packed[:, tile] = block.T.reshape(GROUPS, NEAR, 128)
        departures.append(
            pltpu.make_async_copy(
                packed.at[:, pl.ds(first, end - first)],
                out_ref.at[:, pl.ds(first, end - first)],
                out_sems.at[number],
            )
        )
        departures[-1].start()
    for departure in departures:
        departure.wait()


def derive_line(values, odd_table, even_table, centre):
    sums = [values[k] + values[6 - k] for k in range(3)]
    differences = [values[k] - values[6 - k] for k in range(3)]
    even = [
        sum(float(odd_table[i, j]) * differences[j] for j in range(1, 3))
        + float(odd_table[i, 0]) * differences[0]
        for i in range(4)
    ]
    odd = [
        (float(even_table[i, 0]) * sums[0] + float(even_table[i, 1]) * sums[1])
        + (float(even_table[i, 2]) * sums[2] + float(centre[i]) * values[3])
        for i in range(3)
    ]
    return (
        [even[i] + odd[i] for i in range(3)]
        + [even[3]]
        + [even[i] - odd[i] for i in (2, 1, 0)]
    )


CHUNKS = (0, 7, 13, 19, 25, 31, FIELD_TILES)
BACK_CHUNKS = (0, 5, 10, 15, BACK_TILES)


def main_kernel(
    in_ref,
    metric_hbm,
    synth_ref,
    back_hbm,
    jump_hbm,
    out_ref,
    jump_out,
    metric_ref,
    back_ref,
    sems,
    plane,
    first,
    second,
    product,
    *parts,
):
    metric_copy = pltpu.make_async_copy(metric_hbm, metric_ref, sems.at[3])
    metric_copy.start()
    back_copies = stack_table(back_hbm, back_ref, sems)
    jump_copy = pltpu.make_async_copy(jump_hbm, jump_out, sems.at[4])
    jump_copy.start()
    masks = block_masks()
    matrix = lobatto_matrix(POINTS - 1)
    mirrored = matrix[:, ::-1]
    odd_table = (matrix - mirrored)[:4, :3] / 2.0
    even_table = (matrix + mirrored)[:3, :3] / 2.0
    centre = matrix[:3, 3]

    def gather(chunk):
        for place, tile in enumerate(range(CHUNKS[chunk], CHUNKS[chunk + 1])):
            rows = slice(64 * place, 64 * place + 64)
            for half in range(2):
                swapped = gather_blocks([in_ref[8 * half + k, tile] for k in range(8)], masks)
                upper, lower = split_two(jnp.concatenate(swapped, axis=0))
                parts[chunk][rows, 128 * half : 128 * half + 128] = upper
                parts[chunk][rows, MODES + 128 * half : MODES + 128 * half + 128] = lower

    def synthesize(half, chunk):
        both = parts[chunk][...]
        deep = jnp.concatenate([both, both[:, :MODES]], axis=1)
        rows = slice(64 * CHUNKS[chunk], 64 * CHUNKS[chunk + 1])
        lanes = slice(MODES * half, MODES * half + MODES)
        plane[rows, lanes] = dot(deep, synth_ref[:, lanes])

    def derive(half, field):
        source = slice(MODES * half, MODES * half + 128)
        lanes = slice(128 * half, 128 * half + 128)

        def at(point):
            row = (field * QUAD + point) * 8
            return slice(row, row + 8)

        for line in range(POINTS):
            for stride, base, target in ((1, 7 * line, first), (7, line, second)):
                values = [plane[at(base + stride * k), source] for k in range(POINTS)]
                for k, slope in enumerate(derive_line(values, odd_table, even_table, centre)):
                    target[at(base + stride * k), lanes] = slope

    def combine(half, point):
        east_first, north_first, east_second, north_second = (
            metric_ref[k * QUAD + point] for k in range(4)
        )
        source = slice(MODES * half, MODES * half + 128)
        span = slice(MODES * half + 128, MODES * half + MODES)
        lanes = slice(128 * half, 128 * half + 128)

        def at(field):
            return pl.ds(pl.multiple_of((field * QUAD + point) * 8, 8), 8)

        speed = [plane[at(k), source] for k in range(3)]
        base = [plane[at(3 + k), source] for k in range(3)]
        along = sum(speed[k] * first[at(3 + k), lanes] for k in range(3))
        across = sum(speed[k] * second[at(3 + k), lanes] for k in range(3))
        turned = (
            east_first * along + east_second * across,
            north_first * along + north_second * across,
            sum(speed[k] * plane[at(3 + k), span] for k in range(3)),
        )
        flow_first = base[0] * east_first + base[1] * north_first
        flow_second = base[0] * east_second + base[1] * north_second
        for k in range(3):
            carried = (
                flow_first * first[at(k), lanes]
                + flow_second * second[at(k), lanes]
                + base[2] * plane[at(k), span]
            )
            product[at(k), lanes] = turned[k] - carried

    def analyse(chunk):
        rows = slice(64 * BACK_CHUNKS[chunk], 64 * BACK_CHUNKS[chunk + 1])
        upper, lower = split_two(product[rows, :])
        return dot(jnp.concatenate([upper, lower, upper], axis=1), back_ref[...])

    def scatter(chunk, coefficient):
        for place, tile in enumerate(range(BACK_CHUNKS[chunk], BACK_CHUNKS[chunk + 1])):
            for half in range(2):
                pieces = [
                    coefficient[64 * place + 8 * k : 64 * place + 8 * k + 8, 128 * half : 128 * half + 128]
                    for k in range(8)
                ]
                for k, swapped in enumerate(scatter_blocks(pieces, masks)):
                    out_ref[8 * half + k, tile] = swapped


    product[BACK_ROWS * 8 :, :] = jnp.zeros((BACK_TILES * 64 - BACK_ROWS * 8, MODES), jnp.float32)
    gather(0)
    for chunk in range(6):
        synthesize(0, chunk)
        if chunk < 5:
            gather(chunk + 1)
        if chunk:
            derive(0, chunk - 1)
    for chunk in range(6):
        synthesize(1, chunk)
        if chunk == 0:
            derive(0, 5)
        else:
            derive(1, chunk - 1)
    derive(1, 5)
    metric_copy.wait()
    for copy in back_copies:
        copy.wait()

    @pl.loop(0, QUAD, unroll=4)
    def _(point):
        combine(0, point)
        combine(1, point)
    held = analyse(0)
    for chunk in range(4):
        following = analyse(chunk + 1) if chunk < 3 else None
        scatter(chunk, held)
        held = following
    jump_copy.wait()


def traces_of(adjoint_ref):
    return jnp.concatenate(
        [
            jnp.concatenate(
                [adjoint_ref[component * QUAD + rim_point(side, step)] for side in range(4)], axis=1
            )
            for component in range(3)
            for step in range(POINTS)
        ],
        axis=0,
    )


def fetch(source, target, sem):
    copy = pltpu.make_async_copy(source, target, sem)
    copy.start()
    copy.wait()


def send_kernel(adjoint_hbm, sides_ref, *refs):
    out_refs, (adjoint_ref, sem) = refs[:4], refs[4:]
    fetch(adjoint_hbm, adjoint_ref, sem)
    traces = traces_of(adjoint_ref)
    chosen = lax.broadcasted_iota(jnp.int32, (512, 4 * SLOTS), 0) == sides_ref[...]
    chosen = jnp.where(chosen, 1.0, 0.0).astype(jnp.bfloat16)
    outgoing = sum(dot(part, chosen) for part in split_three(traces))
    padding = jnp.zeros((TRACE_LANES - TRACE_ROWS, 128), jnp.float32)
    outgoing = jnp.concatenate([outgoing, padding], axis=0).T
    for direction, out_ref in enumerate(out_refs):
        out_ref[...] = outgoing[direction * SLOTS : (direction + 1) * SLOTS]


def stack_table(source, target, sems):
    copies = [
        pltpu.make_async_copy(
            source.at[pl.ds(MODES * part, MODES)],
            target.at[pl.ds(MODES * place, MODES)],
            sems.at[place],
        )
        for place, part in enumerate((0, 0, 1))
    ]
    for copy in copies:
        copy.start()
    return copies


def ready_kernel(group_ref, metric_ref, synth_ref, out_ref, synth_out, turned, spread, sems):
    copies = stack_table(synth_ref, synth_out, sems)
    turned[...] = jnp.concatenate(
        [metric_ref[...], jnp.zeros((256 - 4 * QUAD, 128), jnp.float32)], axis=0
    ).T
    own = turned[pl.ds(pl.multiple_of(group_ref[0] * NEAR, NEAR), NEAR), :]
    for index in range(4 * QUAD):
        spread[index] = jnp.broadcast_to(own[:, index : index + 1], (NEAR, 128))
    copies.append(pltpu.make_async_copy(spread, out_ref, sems.at[3]))
    copies[-1].start()
    for copy in copies:
        copy.wait()


def jump_kernel(adjoint_hbm, index_ref, penalty_ref, *refs):
    received_refs, (out_ref, adjoint_ref, held, sem) = refs[:4], refs[4:]
    fetch(adjoint_hbm, adjoint_ref, sem)
    traces = traces_of(adjoint_ref)
    received = jnp.concatenate([ref[...] for ref in received_refs], axis=0).T[:TRACE_ROWS]
    index = index_ref[...]
    where_local = lax.broadcasted_iota(jnp.int32, (512, 128), 0)
    where_far = lax.broadcasted_iota(jnp.int32, (128, 128), 0) + 512
    local_parts = split_three(traces)
    far_parts = split_three(received)
    for side in range(4):
        wanted = index[side : side + 1]
        near = jnp.where(where_local == wanted, 1.0, 0.0).astype(jnp.bfloat16)
        far = jnp.where(where_far == wanted, 1.0, 0.0).astype(jnp.bfloat16)
        outer = sum(dot(part, near) for part in local_parts) + sum(
            dot(part, far) for part in far_parts
        )
        for component in range(3):
            for step in range(POINTS):
                row = (component * POINTS + step) * GROUPS
                far_row = (component * POINTS + 6 - step) * GROUPS
                weight = penalty_ref[side * POINTS + step : side * POINTS + step + 1]
                inner = adjoint_ref[component * QUAD + rim_point(side, step)]
                jump = outer[far_row : far_row + GROUPS] - inner
                held[(component * POINTS + step) * 4 + side] = weight * jump
    fetch(held, out_ref, sem)


BACK_GROUPS = (0, 7, 13, BACK_TILES)


def unpack_kernel(group_ref, in_ref, jump_ref, out_ref, advect, sems):
    turn = group_ref[0] % 8
    sides_at = {}
    for side in range(4):
        for step in range(POINTS):
            sides_at.setdefault(rim_point(side, step), []).append((side, step))
    departures = []
    for component in range(3):
        for tile in range(BACK_GROUPS[component], BACK_GROUPS[component + 1]):
            block = in_ref[:, tile].reshape(128, 128).T
            for k in range(8):
                row = 8 * tile + lax.rem(k - turn + 8, 8)
                advect[row] = block[16 * k : 16 * k + 16]
        first = component * QUAD
        for point, sides in sides_at.items():
            value = advect[first + point]
            for side, step in sides:
                value = value + jump_ref[(component * POINTS + step) * 4 + side]
            advect[first + point] = value
        departures.append(
            pltpu.make_async_copy(
                advect.at[pl.ds(first, QUAD)], out_ref.at[pl.ds(first, QUAD)], sems.at[component]
            )
        )
        departures[-1].start()
    for departure in departures:
        departure.wait()


def call(kernel, outs, *args, places=None, scratch=(), grant=12):
    spaces = {"v": pltpu.VMEM, "V": pltpu.VMEM, "h": pltpu.HBM, "s": pltpu.SMEM}
    places = places or "v" * len(args)
    many = isinstance(outs, list)
    outs = [
        jax.ShapeDtypeStruct(o, jnp.float32) if isinstance(o, tuple) else o
        for o in (outs if many else [outs])
    ]
    out_specs = [
        pl.BlockSpec(memory_space=getattr(o, "memory_space", None) or pltpu.VMEM) for o in outs
    ]
    moved = sum(int(np.prod(a.shape)) * a.dtype.itemsize for a in (*args, *outs))
    args = [
        pltpu.with_memory_space_constraint(a, spaces[p]) if p in "hV" else a
        for a, p in zip(args, places)
    ]
    return pl.pallas_call(
        kernel,
        out_shape=outs if many else outs[0],
        in_specs=[pl.BlockSpec(memory_space=spaces[p]) for p in places],
        out_specs=out_specs if many else out_specs[0],
        scratch_shapes=list(scratch),
        compiler_params=pltpu.CompilerParams(vmem_limit_bytes=grant * MEBI),
        cost_estimate=pl.CostEstimate(flops=0, bytes_accessed=moved, transcendentals=0),
    )(*args)


def passed_along(block, axis, distance):
    count = lax.axis_size(axis)
    return lax.ppermute(block, axis, [((i - distance) % count, i) for i in range(count)])


def shards(adjoint, base_flow, metric, penalty, send_sides, ext_index):
    synthesis, analysis, slope = fourier_tables()
    by_half = np.arange(2 * MODES).reshape(2, 2, 128).transpose(1, 0, 2).reshape(-1)
    synth = stacked(np.concatenate([synthesis, slope], axis=0)[by_half].T)
    back = stacked(analysis.T)
    natural = jnp.transpose(adjoint, (0, 2, 1, 3)).reshape(BACK_ROWS, GROUPS, 128)
    base = jnp.transpose(base_flow, (0, 2, 1, 3)).reshape(BACK_ROWS, GROUPS, 128)
    group = lax.axis_index("mode").reshape(1)

    packed = call(
        pack_kernel,
        pltpu.HBM((GROUPS, FIELD_TILES, NEAR, 128), jnp.float32),
        group,
        natural,
        base,
        places="shh",
        scratch=[
            pltpu.VMEM((8 * FIELD_TILES, GROUPS, 128), jnp.float32),
            pltpu.VMEM((GROUPS, FIELD_TILES, NEAR, 128), jnp.float32),
            pltpu.SemaphoreType.DMA((7,)),
            pltpu.SemaphoreType.DMA((7,)),
        ],
    )
    arrived = lax.all_to_all(packed, "mode", split_axis=0, concat_axis=0, tiled=True)

    outgoing = call(
        send_kernel,
        [(SLOTS, TRACE_LANES)] * 4,
        natural,
        send_sides.reshape(1, 4 * SLOTS),
        places="hv",
        scratch=[
            pltpu.VMEM((BACK_ROWS, GROUPS, 128), jnp.float32),
            pltpu.SemaphoreType.DMA(()),
        ],
    )
    received = [passed_along(block, "elem", o) for block, o in zip(outgoing, OFFSETS)]
    own_metric, synth = call(
        ready_kernel,
        [
            pltpu.HBM((4 * QUAD, NEAR, 128), jnp.float32),
            pltpu.VMEM((3 * MODES, 2 * MODES), jnp.bfloat16),
        ],
        group,
        metric.reshape(4 * QUAD, 128),
        jnp.asarray(synth),
        places="svh",
        scratch=[
            pltpu.VMEM((128, 256), jnp.float32),
            pltpu.VMEM((4 * QUAD, NEAR, 128), jnp.float32),
            pltpu.SemaphoreType.DMA((4,)),
        ],
    )
    jumps = call(
        jump_kernel,
        pltpu.HBM((84, GROUPS, 128), jnp.float32),
        natural,
        ext_index,
        penalty.reshape(4 * POINTS, 128),
        *received,
        places="hvvvvvv",
        scratch=[
            pltpu.VMEM((BACK_ROWS, GROUPS, 128), jnp.float32),
            pltpu.VMEM((84, GROUPS, 128), jnp.float32),
            pltpu.SemaphoreType.DMA(()),
        ],
    )

    coefficients, jumps = call(
        main_kernel,
        [(GROUPS, BACK_TILES, NEAR, 128), pltpu.VMEM((84, GROUPS, 128), jnp.float32)],
        arrived,
        own_metric,
        synth,
        jnp.asarray(back),
        jumps,
        places="Vhvhh",
        scratch=[
            pltpu.VMEM((4 * QUAD, NEAR, 128), jnp.float32),
            pltpu.VMEM((3 * MODES, MODES), jnp.bfloat16),
            pltpu.SemaphoreType.DMA((5,)),
            pltpu.VMEM((64 * FIELD_TILES, 2 * MODES), jnp.float32),
            pltpu.VMEM((8 * ROWS, MODES), jnp.float32),
            pltpu.VMEM((8 * ROWS, MODES), jnp.float32),
            pltpu.VMEM((64 * BACK_TILES, MODES), jnp.float32),
        ]
        + [
            pltpu.VMEM((64 * (end - first), 2 * MODES), jnp.bfloat16)
            for first, end in zip(CHUNKS, CHUNKS[1:])
        ],
        grant=28,
    )
    returned = lax.all_to_all(coefficients, "mode", split_axis=0, concat_axis=0, tiled=True)
    out = call(
        unpack_kernel,
        pltpu.HBM((BACK_ROWS, GROUPS, 128), jnp.float32),
        group,
        returned,
        jumps,
        places="svv",
        scratch=[
            pltpu.VMEM((8 * BACK_TILES, GROUPS, 128), jnp.float32),
            pltpu.SemaphoreType.DMA((3,)),
        ],
    )
    return jnp.transpose(out.reshape(3, QUAD, GROUPS, 128), (0, 2, 1, 3))


def solution(mesh):
    placed = (
        P(None, "mode", None, "elem"),
        P(None, "mode", None, "elem"),
        P(None, None, "elem"),
        P(None, None, "elem"),
        P("elem", None, None),
        P(None, "elem"),
    )
    return jax.shard_map(
        shards, mesh=mesh, in_specs=placed, out_specs=P(None, "mode", None, "elem"), check_vma=False
    )
```

```python
import math

import jax
import jax.numpy as jnp
import numpy as np
from jax import lax
from jax.experimental import pallas as pl
from jax.experimental.pallas import tpu as pltpu
from jax.sharding import PartitionSpec as P

MODES = 256
POINTS = 7
QUAD = 49
GROUPS = 16
NEAR = 8
ROWS = 6 * QUAD
FIELD_TILES = 37
BACK_ROWS = 3 * QUAD
BACK_TILES = 19
SLOTS = 32
OFFSETS = (1, -1, 2, -2)
TRACE_ROWS = 3 * POINTS * GROUPS
TRACE_LANES = 384
MEBI = 1024 * 1024


def legendre_pair(degree, position):
    previous = 1.0
    current = position
    for order_index in range(2, degree + 1):
        following = (
            (2 * order_index - 1) * position * current - (order_index - 1) * previous
        ) / order_index
        previous = current
        current = following
    return (current, previous)


def lobatto_points(degree):
    node_list = []
    for point_index in range(degree + 1):
        estimate = -math.cos(math.pi * point_index / degree)
        for newton_step in range(60):
            current, previous = legendre_pair(degree, estimate)
            estimate = estimate - (estimate * current - previous) / ((degree + 1) * current)
        node_list.append(estimate)
    node_list[0] = -1.0
    node_list[degree] = 1.0
    return node_list


def lobatto_matrix(degree):
    nodes = lobatto_points(degree)
    at_nodes = [legendre_pair(degree, value)[0] for value in nodes]
    count = degree + 1
    matrix = np.zeros((count, count))
    for row in range(count):
        for col in range(count):
            if row != col:
                matrix[row, col] = at_nodes[row] / (at_nodes[col] * (nodes[row] - nodes[col]))
    matrix[0, 0] = -degree * (degree + 1) / 4.0
    matrix[degree, degree] = degree * (degree + 1) / 4.0
    return matrix


def fourier_tables():
    planes = np.arange(MODES)[:, None]
    slot = np.arange(MODES)[None, :]
    wavenumber = slot // 2
    angles = (wavenumber * planes % MODES) * (2.0 * math.pi / MODES)
    synthesis = np.where(slot % 2 == 1, -np.sin(angles), np.cos(angles))
    synthesis = np.where(slot == 1, np.where(planes % 2 == 0, 1.0, -1.0), synthesis)
    weights = np.where(slot < 2, 1.0, 2.0) / MODES
    analysis = (synthesis * weights).T
    rates = wavenumber * (4.0 / MODES)
    slope = np.zeros((MODES, MODES))
    slope[:, 0::2] = rates[:, 0::2] * synthesis[:, 1::2]
    slope[:, 1::2] = -rates[:, 0::2] * synthesis[:, 0::2]
    return synthesis, analysis, slope


def stacked(table):
    table = table.astype(np.float32)
    high = table.astype(jnp.bfloat16)
    low = (table - high.astype(np.float32)).astype(jnp.bfloat16)
    return np.concatenate([high, low], axis=0)


def rim_point(side, step):
    last = POINTS - 1
    return (step, POINTS * step + last, POINTS * last + last - step, POINTS * (last - step))[side]


def barrel(turned, masks):
    moved = [turned[-k % 8] for k in range(8)]
    for bit in range(3):
        moved = [jnp.where(masks[bit], moved[(k - (1 << bit)) % 8], moved[k]) for k in range(8)]
    return moved


def gather_blocks(turned, masks):
    return [
        pltpu.roll(tile, 128 - 16 * g, 1) if g else tile
        for g, tile in enumerate(barrel(turned, masks))
    ]


def scatter_blocks(tiles, masks):
    return barrel([pltpu.roll(tile, 16 * q, 1) if q else tile for q, tile in enumerate(tiles)], masks)


def block_masks():
    block = lax.broadcasted_iota(jnp.int32, (8, 128), 1) // 16
    return [(block & (1 << bit)) != 0 for bit in range(3)]


def split_two(value):
    high = value.astype(jnp.bfloat16)
    low = (value - high.astype(jnp.float32)).astype(jnp.bfloat16)
    return high, low


def split_three(value):
    high = value.astype(jnp.bfloat16)
    rest = value - high.astype(jnp.float32)
    middle = rest.astype(jnp.bfloat16)
    low = (rest - middle.astype(jnp.float32)).astype(jnp.bfloat16)
    return high, middle, low


def dot(left, right):
    return jnp.dot(left, right, preferred_element_type=jnp.float32)


ADJOINT_CUTS = (0, 48, 96, BACK_ROWS)
BASE_CUTS = (0, 48, 96, 128, BACK_ROWS)
PACK_GROUPS = (0, 6, 12, 18, 24, 30, 34, FIELD_TILES)


def pack_kernel(
    group_ref,
    adjoint_ref,
    base_ref,
    sides_ref,
    metric_ref,
    synth_hbm,
    out_ref,
    trace_out,
    metric_out,
    synth_out,
    fields,
    packed,
    turned,
    spread,
    in_sems,
    out_sems,
    table_sems,
):
    arrivals = []
    sources = ((adjoint_ref, 0, ADJOINT_CUTS), (base_ref, BACK_ROWS, BASE_CUTS))
    for source, offset, cuts in sources:
        for first, end in zip(cuts, cuts[1:]):
            arrivals.append(
                pltpu.make_async_copy(
                    source.at[pl.ds(first, end - first)],
                    fields.at[pl.ds(offset + first, end - first)],
                    in_sems.at[len(arrivals)],
                )
            )
            arrivals[-1].start()
    tables = stack_table(synth_hbm, synth_out, table_sems)
    fields[ROWS:] = jnp.zeros((8 * FIELD_TILES - ROWS, GROUPS, 128), jnp.float32)
    spread_metric(group_ref, metric_ref, turned, spread)
    metric_copy = pltpu.make_async_copy(spread, metric_out, table_sems.at[3])
    metric_copy.start()
    turn = group_ref[0] % 8
    order = [lax.rem(k - turn + 8, 8) for k in range(8)]
    departures = []
    for number, (first, end) in enumerate(zip(PACK_GROUPS, PACK_GROUPS[1:])):
        arrivals[number].wait()
        for tile in range(first, end):
            block = jnp.concatenate([fields[8 * tile + k] for k in order], axis=0)
            packed[:, tile] = block.T.reshape(GROUPS, NEAR, 128)
        departures.append(
            pltpu.make_async_copy(
                packed.at[:, pl.ds(first, end - first)],
                out_ref.at[:, pl.ds(first, end - first)],
                out_sems.at[number],
            )
        )
        departures[-1].start()
        if number == 2:
            outgoing_traces(fields, sides_ref, trace_out)
    for departure in (*departures, *tables, metric_copy):
        departure.wait()


def derive_line(values, odd_table, even_table, centre):
    sums = [values[k] + values[6 - k] for k in range(3)]
    differences = [values[k] - values[6 - k] for k in range(3)]
    even = [
        sum(float(odd_table[i, j]) * differences[j] for j in range(1, 3))
        + float(odd_table[i, 0]) * differences[0]
        for i in range(4)
    ]
    odd = [
        (float(even_table[i, 0]) * sums[0] + float(even_table[i, 1]) * sums[1])
        + (float(even_table[i, 2]) * sums[2] + float(centre[i]) * values[3])
        for i in range(3)
    ]
    return (
        [even[i] + odd[i] for i in range(3)]
        + [even[3]]
        + [even[i] - odd[i] for i in (2, 1, 0)]
    )


CHUNKS = (0, 7, 13, 19, 25, 31, FIELD_TILES)
BACK_CHUNKS = (0, 5, 10, 15, BACK_TILES)


def main_kernel(
    in_ref,
    metric_hbm,
    synth_ref,
    back_hbm,
    trace_hbm,
    out_hbm,
    trace_out_0,
    trace_out_1,
    trace_out_2,
    trace_out_3,
    metric_ref,
    back_ref,
    out_ref,
    sems,
    out_sems,
    plane,
    first,
    second,
    product,
    *parts,
):
    metric_copy = pltpu.make_async_copy(metric_hbm, metric_ref, sems.at[3])
    metric_copy.start()
    back_copies = stack_table(back_hbm, back_ref, sems)
    departures = [
        pltpu.make_async_copy(trace_hbm.at[pl.ds(SLOTS * d, SLOTS)], target, out_sems.at[d])
        for d, target in enumerate((trace_out_0, trace_out_1, trace_out_2, trace_out_3))
    ]
    for departure in departures:
        departure.start()
    masks = block_masks()
    matrix = lobatto_matrix(POINTS - 1)
    mirrored = matrix[:, ::-1]
    odd_table = (matrix - mirrored)[:4, :3] / 2.0
    even_table = (matrix + mirrored)[:3, :3] / 2.0
    centre = matrix[:3, 3]

    def gather(chunk):
        for place, tile in enumerate(range(CHUNKS[chunk], CHUNKS[chunk + 1])):
            rows = slice(64 * place, 64 * place + 64)
            for half in range(2):
                swapped = gather_blocks([in_ref[8 * half + k, tile] for k in range(8)], masks)
                upper, lower = split_two(jnp.concatenate(swapped, axis=0))
                parts[chunk][rows, 128 * half : 128 * half + 128] = upper
                parts[chunk][rows, MODES + 128 * half : MODES + 128 * half + 128] = lower

    def synthesize(half, chunk):
        both = parts[chunk][...]
        deep = jnp.concatenate([both, both[:, :MODES]], axis=1)
        rows = slice(64 * CHUNKS[chunk], 64 * CHUNKS[chunk + 1])
        lanes = slice(MODES * half, MODES * half + MODES)
        plane[rows, lanes] = dot(deep, synth_ref[:, lanes])

    def derive(half, field):
        source = slice(MODES * half, MODES * half + 128)
        lanes = slice(128 * half, 128 * half + 128)

        def at(point):
            row = (field * QUAD + point) * 8
            return slice(row, row + 8)

        for line in range(POINTS):
            for stride, base, target in ((1, 7 * line, first), (7, line, second)):
                values = [plane[at(base + stride * k), source] for k in range(POINTS)]
                for k, slope in enumerate(derive_line(values, odd_table, even_table, centre)):
                    target[at(base + stride * k), lanes] = slope

    def combine(half, point):
        east_first, north_first, east_second, north_second = (
            metric_ref[point * 4 + k] for k in range(4)
        )
        source = slice(MODES * half, MODES * half + 128)
        span = slice(MODES * half + 128, MODES * half + MODES)
        lanes = slice(128 * half, 128 * half + 128)

        def at(field):
            return pl.ds(pl.multiple_of((field * QUAD + point) * 8, 8), 8)

        speed = [plane[at(k), source] for k in range(3)]
        base = [plane[at(3 + k), source] for k in range(3)]
        along = sum(speed[k] * first[at(3 + k), lanes] for k in range(3))
        across = sum(speed[k] * second[at(3 + k), lanes] for k in range(3))
        turned = (
            east_first * along + east_second * across,
            north_first * along + north_second * across,
            sum(speed[k] * plane[at(3 + k), span] for k in range(3)),
        )
        flow_first = base[0] * east_first + base[1] * north_first
        flow_second = base[0] * east_second + base[1] * north_second
        for k in range(3):
            carried = (
                flow_first * first[at(k), lanes]
                + flow_second * second[at(k), lanes]
                + base[2] * plane[at(k), span]
            )
            product[at(k), lanes] = turned[k] - carried

    def analyse(chunk):
        rows = slice(64 * BACK_CHUNKS[chunk], 64 * BACK_CHUNKS[chunk + 1])
        upper, lower = split_two(product[rows, :])
        return dot(jnp.concatenate([upper, lower, upper], axis=1), back_ref[...])

    def scatter(chunk, coefficient):
        for place, tile in enumerate(range(BACK_CHUNKS[chunk], BACK_CHUNKS[chunk + 1])):
            for half in range(2):
                pieces = [
                    coefficient[64 * place + 8 * k : 64 * place + 8 * k + 8, 128 * half : 128 * half + 128]
                    for k in range(8)
                ]
                for k, swapped in enumerate(scatter_blocks(pieces, masks)):
                    out_ref[8 * half + k, tile] = swapped


    product[BACK_ROWS * 8 :, :] = jnp.zeros((BACK_TILES * 64 - BACK_ROWS * 8, MODES), jnp.float32)
    gather(0)
    for chunk in range(6):
        synthesize(0, chunk)
        if chunk < 5:
            gather(chunk + 1)
        if chunk:
            derive(0, chunk - 1)
    for chunk in range(6):
        synthesize(1, chunk)
        if chunk == 0:
            derive(0, 5)
        else:
            derive(1, chunk - 1)
    derive(1, 5)
    metric_copy.wait()
    for copy in back_copies:
        copy.wait()

    @pl.loop(0, QUAD, unroll=4)
    def _(point):
        combine(0, point)
        combine(1, point)
    held = analyse(0)
    for chunk in range(4):
        following = analyse(chunk + 1) if chunk < 3 else None
        scatter(chunk, held)
        held = following
        tiles = pl.ds(BACK_CHUNKS[chunk], BACK_CHUNKS[chunk + 1] - BACK_CHUNKS[chunk])
        departures.append(
            pltpu.make_async_copy(out_ref.at[:, tiles], out_hbm.at[:, tiles], out_sems.at[4 + chunk])
        )
        departures[-1].start()
    for departure in departures:
        departure.wait()


def traces_of(adjoint_ref):
    return jnp.concatenate(
        [
            jnp.concatenate(
                [adjoint_ref[component * QUAD + rim_point(side, step)] for side in range(4)], axis=1
            )
            for component in range(3)
            for step in range(POINTS)
        ],
        axis=0,
    )


def fetch(source, target, sem):
    copy = pltpu.make_async_copy(source, target, sem)
    copy.start()
    copy.wait()


def outgoing_traces(adjoint_ref, sides_ref, out_ref):
    sides = jnp.concatenate([sides_ref[d : d + 1] for d in range(4)], axis=1)
    chosen = lax.broadcasted_iota(jnp.int32, (512, 4 * SLOTS), 0) == sides
    chosen = jnp.where(chosen, 1.0, 0.0).astype(jnp.bfloat16)
    outgoing = sum(dot(part, chosen) for part in split_three(traces_of(adjoint_ref)))
    padding = jnp.zeros((TRACE_LANES - TRACE_ROWS, 128), jnp.float32)
    out_ref[...] = jnp.concatenate([outgoing, padding], axis=0).T


def stack_table(source, target, sems):
    copies = [
        pltpu.make_async_copy(
            source.at[pl.ds(MODES * part, MODES)],
            target.at[pl.ds(MODES * place, MODES)],
            sems.at[place],
        )
        for place, part in enumerate((0, 0, 1))
    ]
    for copy in copies:
        copy.start()
    return copies


def spread_metric(group_ref, metric_ref, turned, spread):
    rows = [metric_ref[point] for point in range(QUAD)]
    turned[...] = jnp.concatenate(
        rows + [jnp.zeros((256 - 4 * QUAD, 128), jnp.float32)], axis=0
    ).T
    own = turned[pl.ds(pl.multiple_of(group_ref[0] * NEAR, NEAR), NEAR), :]
    for index in range(4 * QUAD):
        spread[index] = jnp.broadcast_to(own[:, index : index + 1], (NEAR, 128))


def jump_kernel(adjoint_hbm, index_ref, penalty_ref, *refs):
    received_refs, (out_ref, adjoint_ref, sem) = refs[:4], refs[4:]
    fetch(adjoint_hbm, adjoint_ref, sem)
    traces = traces_of(adjoint_ref)
    received = jnp.concatenate([ref[...] for ref in received_refs], axis=0).T[:TRACE_ROWS]
    index = index_ref[...]
    where_local = lax.broadcasted_iota(jnp.int32, (512, 128), 0)
    where_far = lax.broadcasted_iota(jnp.int32, (128, 128), 0) + 512
    local_parts = split_three(traces)
    far_parts = split_three(received)
    for side in range(4):
        wanted = index[side : side + 1]
        near = jnp.where(where_local == wanted, 1.0, 0.0).astype(jnp.bfloat16)
        far = jnp.where(where_far == wanted, 1.0, 0.0).astype(jnp.bfloat16)
        outer = sum(dot(part, near) for part in local_parts) + sum(
            dot(part, far) for part in far_parts
        )
        for component in range(3):
            for step in range(POINTS):
                row = (component * POINTS + step) * GROUPS
                far_row = (component * POINTS + 6 - step) * GROUPS
                weight = penalty_ref[side * POINTS + step : side * POINTS + step + 1]
                inner = adjoint_ref[component * QUAD + rim_point(side, step)]
                jump = outer[far_row : far_row + GROUPS] - inner
                out_ref[(component * POINTS + step) * 4 + side] = weight * jump


BACK_GROUPS = (0, 7, 13, BACK_TILES)


def unpack_kernel(group_ref, in_ref, jump_ref, out_ref, advect, sems):
    turn = group_ref[0] % 8
    sides_at = {}
    for side in range(4):
        for step in range(POINTS):
            sides_at.setdefault(rim_point(side, step), []).append((side, step))
    departures = []
    for component in range(3):
        for tile in range(BACK_GROUPS[component], BACK_GROUPS[component + 1]):
            block = in_ref[:, tile].reshape(128, 128).T
            for k in range(8):
                row = 8 * tile + lax.rem(k - turn + 8, 8)
                advect[row] = block[16 * k : 16 * k + 16]
        first = component * QUAD
        for point, sides in sides_at.items():
            value = advect[first + point]
            for side, step in sides:
                value = value + jump_ref[(component * POINTS + step) * 4 + side]
            advect[first + point] = value
        departures.append(
            pltpu.make_async_copy(
                advect.at[pl.ds(first, QUAD)], out_ref.at[pl.ds(first, QUAD)], sems.at[component]
            )
        )
        departures[-1].start()
    for departure in departures:
        departure.wait()


def call(kernel, outs, *args, places=None, scratch=(), grant=12):
    spaces = {"v": pltpu.VMEM, "V": pltpu.VMEM, "h": pltpu.HBM, "s": pltpu.SMEM}
    places = places or "v" * len(args)
    many = isinstance(outs, list)
    outs = [
        jax.ShapeDtypeStruct(o, jnp.float32) if isinstance(o, tuple) else o
        for o in (outs if many else [outs])
    ]
    out_specs = [
        pl.BlockSpec(memory_space=getattr(o, "memory_space", None) or pltpu.VMEM) for o in outs
    ]
    moved = sum(int(np.prod(a.shape)) * a.dtype.itemsize for a in (*args, *outs))
    args = [
        pltpu.with_memory_space_constraint(a, spaces[p]) if p in "hV" else a
        for a, p in zip(args, places)
    ]
    return pl.pallas_call(
        kernel,
        out_shape=outs if many else outs[0],
        in_specs=[pl.BlockSpec(memory_space=spaces[p]) for p in places],
        out_specs=out_specs if many else out_specs[0],
        scratch_shapes=list(scratch),
        compiler_params=pltpu.CompilerParams(vmem_limit_bytes=grant * MEBI),
        cost_estimate=pl.CostEstimate(flops=0, bytes_accessed=moved, transcendentals=0),
    )(*args)


def passed_along(block, axis, distance):
    count = lax.axis_size(axis)
    return lax.ppermute(block, axis, [((i - distance) % count, i) for i in range(count)])


def shards(adjoint, base_flow, metric, penalty, send_sides, ext_index):
    synthesis, analysis, slope = fourier_tables()
    by_half = np.arange(2 * MODES).reshape(2, 2, 128).transpose(1, 0, 2).reshape(-1)
    synth = stacked(np.concatenate([synthesis, slope], axis=0)[by_half].T)
    back = stacked(analysis.T)
    natural = jnp.transpose(adjoint, (0, 2, 1, 3)).reshape(BACK_ROWS, GROUPS, 128)
    base = jnp.transpose(base_flow, (0, 2, 1, 3)).reshape(BACK_ROWS, GROUPS, 128)
    group = lax.axis_index("mode").reshape(1)

    f32, bf16 = jnp.float32, jnp.bfloat16
    packed, traces, own_metric, synth = call(
        pack_kernel,
        [
            pltpu.HBM((GROUPS, FIELD_TILES, NEAR, 128), f32),
            (4 * SLOTS, TRACE_LANES),
            pltpu.HBM((4 * QUAD, NEAR, 128), f32),
            pltpu.VMEM((3 * MODES, 2 * MODES), bf16),
        ],
        group,
        natural,
        base,
        send_sides.reshape(4, SLOTS),
        jnp.transpose(metric, (1, 0, 2)),
        jnp.asarray(synth),
        places="shhvvh",
        scratch=[
            pltpu.VMEM((8 * FIELD_TILES, GROUPS, 128), f32),
            pltpu.VMEM((GROUPS, FIELD_TILES, NEAR, 128), f32),
            pltpu.VMEM((128, 256), f32),
            pltpu.VMEM((4 * QUAD, NEAR, 128), f32),
            pltpu.SemaphoreType.DMA((7,)),
            pltpu.SemaphoreType.DMA((7,)),
            pltpu.SemaphoreType.DMA((4,)),
        ],
        grant=16,
    )
    arrived = lax.all_to_all(packed, "mode", split_axis=0, concat_axis=0, tiled=True)
    coefficients, *outgoing = call(
        main_kernel,
        [pltpu.HBM((GROUPS, BACK_TILES, NEAR, 128), f32)]
        + [pltpu.HBM((SLOTS, TRACE_LANES), f32)] * 4,
        arrived,
        own_metric,
        synth,
        jnp.asarray(back),
        traces,
        places="Vhvhh",
        scratch=[
            pltpu.VMEM((4 * QUAD, NEAR, 128), f32),
            pltpu.VMEM((3 * MODES, MODES), bf16),
            pltpu.VMEM((GROUPS, BACK_TILES, NEAR, 128), f32),
            pltpu.SemaphoreType.DMA((4,)),
            pltpu.SemaphoreType.DMA((8,)),
            pltpu.VMEM((64 * FIELD_TILES, 2 * MODES), f32),
            pltpu.VMEM((8 * ROWS, MODES), f32),
            pltpu.VMEM((8 * ROWS, MODES), f32),
            pltpu.VMEM((64 * BACK_TILES, MODES), f32),
        ]
        + [
            pltpu.VMEM((64 * (end - first), 2 * MODES), bf16)
            for first, end in zip(CHUNKS, CHUNKS[1:])
        ],
        grant=28,
    )
    returned = lax.all_to_all(coefficients, "mode", split_axis=0, concat_axis=0, tiled=True)
    received = [passed_along(block, "elem", o) for block, o in zip(outgoing, OFFSETS)]
    jumps = call(
        jump_kernel,
        (84, GROUPS, 128),
        natural,
        ext_index,
        penalty.reshape(4 * POINTS, 128),
        *received,
        places="hvvvvvv",
        scratch=[pltpu.VMEM((BACK_ROWS, GROUPS, 128), f32), pltpu.SemaphoreType.DMA(())],
    )
    out = call(
        unpack_kernel,
        pltpu.HBM((BACK_ROWS, GROUPS, 128), jnp.float32),
        group,
        returned,
        jumps,
        places="svv",
        scratch=[
            pltpu.VMEM((8 * BACK_TILES, GROUPS, 128), f32),
            pltpu.SemaphoreType.DMA((3,)),
        ],
    )
    return jnp.transpose(out.reshape(3, QUAD, GROUPS, 128), (0, 2, 1, 3))


def solution(mesh):
    placed = (
        P(None, "mode", None, "elem"),
        P(None, "mode", None, "elem"),
        P(None, None, "elem"),
        P(None, None, "elem"),
        P("elem", None, None),
        P(None, "elem"),
    )
    return jax.shard_map(
        shards, mesh=mesh, in_specs=placed, out_specs=P(None, "mode", None, "elem"), check_vma=False
    )
```

```python
import math

import jax
import jax.numpy as jnp
import numpy as np
from jax import lax
from jax.experimental import pallas as pl
from jax.experimental.pallas import tpu as pltpu
from jax.sharding import PartitionSpec as P

MODES = 256
POINTS = 7
QUAD = 49
GROUPS = 16
NEAR = 8
ROWS = 6 * QUAD
FIELD_TILES = 37
BACK_ROWS = 3 * QUAD
BACK_TILES = 19
SLOTS = 32
OFFSETS = (1, -1, 2, -2)
TRACE_ROWS = 3 * POINTS * GROUPS
TRACE_LANES = 384
MEBI = 1024 * 1024


def legendre_pair(degree, position):
    previous = 1.0
    current = position
    for order_index in range(2, degree + 1):
        following = (
            (2 * order_index - 1) * position * current - (order_index - 1) * previous
        ) / order_index
        previous = current
        current = following
    return (current, previous)


def lobatto_points(degree):
    node_list = []
    for point_index in range(degree + 1):
        estimate = -math.cos(math.pi * point_index / degree)
        for newton_step in range(60):
            current, previous = legendre_pair(degree, estimate)
            estimate = estimate - (estimate * current - previous) / ((degree + 1) * current)
        node_list.append(estimate)
    node_list[0] = -1.0
    node_list[degree] = 1.0
    return node_list


def lobatto_matrix(degree):
    nodes = lobatto_points(degree)
    at_nodes = [legendre_pair(degree, value)[0] for value in nodes]
    count = degree + 1
    matrix = np.zeros((count, count))
    for row in range(count):
        for col in range(count):
            if row != col:
                matrix[row, col] = at_nodes[row] / (at_nodes[col] * (nodes[row] - nodes[col]))
    matrix[0, 0] = -degree * (degree + 1) / 4.0
    matrix[degree, degree] = degree * (degree + 1) / 4.0
    return matrix


def fourier_tables():
    planes = np.arange(MODES)[:, None]
    slot = np.arange(MODES)[None, :]
    wavenumber = slot // 2
    angles = (wavenumber * planes % MODES) * (2.0 * math.pi / MODES)
    synthesis = np.where(slot % 2 == 1, -np.sin(angles), np.cos(angles))
    synthesis = np.where(slot == 1, np.where(planes % 2 == 0, 1.0, -1.0), synthesis)
    weights = np.where(slot < 2, 1.0, 2.0) / MODES
    analysis = (synthesis * weights).T
    rates = wavenumber * (4.0 / MODES)
    slope = np.zeros((MODES, MODES))
    slope[:, 0::2] = rates[:, 0::2] * synthesis[:, 1::2]
    slope[:, 1::2] = -rates[:, 0::2] * synthesis[:, 0::2]
    return synthesis, analysis, slope


def stacked(table):
    table = table.astype(np.float32)
    high = table.astype(jnp.bfloat16)
    low = (table - high.astype(np.float32)).astype(jnp.bfloat16)
    return np.concatenate([high, low], axis=0)


def rim_point(side, step):
    last = POINTS - 1
    return (step, POINTS * step + last, POINTS * last + last - step, POINTS * (last - step))[side]


def barrel(turned, masks):
    moved = [turned[-k % 8] for k in range(8)]
    for bit in range(3):
        moved = [jnp.where(masks[bit], moved[(k - (1 << bit)) % 8], moved[k]) for k in range(8)]
    return moved


def gather_blocks(turned, masks):
    return [
        pltpu.roll(tile, 128 - 16 * g, 1) if g else tile
        for g, tile in enumerate(barrel(turned, masks))
    ]


def scatter_blocks(tiles, masks):
    return barrel([pltpu.roll(tile, 16 * q, 1) if q else tile for q, tile in enumerate(tiles)], masks)


def block_masks():
    block = lax.broadcasted_iota(jnp.int32, (8, 128), 1) // 16
    return [(block & (1 << bit)) != 0 for bit in range(3)]


def split_two(value):
    high = value.astype(jnp.bfloat16)
    low = (value - high.astype(jnp.float32)).astype(jnp.bfloat16)
    return high, low


def split_three(value):
    high = value.astype(jnp.bfloat16)
    rest = value - high.astype(jnp.float32)
    middle = rest.astype(jnp.bfloat16)
    low = (rest - middle.astype(jnp.float32)).astype(jnp.bfloat16)
    return high, middle, low


def dot(left, right):
    return jnp.dot(left, right, preferred_element_type=jnp.float32)


ADJOINT_CUTS = (0, 48, 96, BACK_ROWS)
BASE_CUTS = (0, 48, 96, 128, BACK_ROWS)
PACK_GROUPS = (0, 6, 12, 18, 24, 30, 34, FIELD_TILES)


def pack_kernel(
    group_ref,
    adjoint_ref,
    base_ref,
    sides_hbm,
    metric_hbm,
    synth_hbm,
    out_ref,
    trace_out,
    metric_out,
    synth_out,
    fields,
    packed,
    turned,
    spread,
    sides_ref,
    metric_ref,
    in_sems,
    out_sems,
    table_sems,
):
    small = (
        pltpu.make_async_copy(metric_hbm, metric_ref, table_sems.at[4]),
        pltpu.make_async_copy(sides_hbm, sides_ref, table_sems.at[5]),
    )
    for copy in small:
        copy.start()
    arrivals = []
    sources = ((adjoint_ref, 0, ADJOINT_CUTS), (base_ref, BACK_ROWS, BASE_CUTS))
    for source, offset, cuts in sources:
        for first, end in zip(cuts, cuts[1:]):
            arrivals.append(
                pltpu.make_async_copy(
                    source.at[pl.ds(first, end - first)],
                    fields.at[pl.ds(offset + first, end - first)],
                    in_sems.at[len(arrivals)],
                )
            )
            arrivals[-1].start()
    tables = stack_table(synth_hbm, synth_out, table_sems)
    fields[ROWS:] = jnp.zeros((8 * FIELD_TILES - ROWS, GROUPS, 128), jnp.float32)
    for copy in small:
        copy.wait()
    spread_metric(group_ref, metric_ref, turned, spread)
    metric_copy = pltpu.make_async_copy(spread, metric_out, table_sems.at[3])
    metric_copy.start()
    turn = group_ref[0] % 8
    order = [lax.rem(k - turn + 8, 8) for k in range(8)]
    departures = []
    for number, (first, end) in enumerate(zip(PACK_GROUPS, PACK_GROUPS[1:])):
        arrivals[number].wait()
        for tile in range(first, end):
            block = jnp.concatenate([fields[8 * tile + k] for k in order], axis=0)
            packed[:, tile] = block.T.reshape(GROUPS, NEAR, 128)
        departures.append(
            pltpu.make_async_copy(
                packed.at[:, pl.ds(first, end - first)],
                out_ref.at[:, pl.ds(first, end - first)],
                out_sems.at[number],
            )
        )
        departures[-1].start()
        if number == 2:
            outgoing_traces(fields, sides_ref, trace_out)
    for departure in (*departures, *tables, metric_copy):
        departure.wait()


def derive_line(values, odd_table, even_table, centre):
    sums = [values[k] + values[6 - k] for k in range(3)]
    differences = [values[k] - values[6 - k] for k in range(3)]
    even = [
        sum(float(odd_table[i, j]) * differences[j] for j in range(1, 3))
        + float(odd_table[i, 0]) * differences[0]
        for i in range(4)
    ]
    odd = [
        (float(even_table[i, 0]) * sums[0] + float(even_table[i, 1]) * sums[1])
        + (float(even_table[i, 2]) * sums[2] + float(centre[i]) * values[3])
        for i in range(3)
    ]
    return (
        [even[i] + odd[i] for i in range(3)]
        + [even[3]]
        + [even[i] - odd[i] for i in (2, 1, 0)]
    )


CHUNKS = (0, 7, 13, 19, 25, 31, FIELD_TILES)
BACK_CHUNKS = (0, 5, 10, 15, BACK_TILES)


def main_kernel(
    in_ref,
    metric_hbm,
    synth_ref,
    back_hbm,
    trace_hbm,
    out_hbm,
    trace_out_0,
    trace_out_1,
    trace_out_2,
    trace_out_3,
    metric_ref,
    back_ref,
    out_ref,
    sems,
    out_sems,
    plane,
    first,
    second,
    product,
    *parts,
):
    metric_copy = pltpu.make_async_copy(metric_hbm, metric_ref, sems.at[3])
    metric_copy.start()
    back_copies = stack_table(back_hbm, back_ref, sems)
    departures = [
        pltpu.make_async_copy(trace_hbm.at[pl.ds(SLOTS * d, SLOTS)], target, out_sems.at[d])
        for d, target in enumerate((trace_out_0, trace_out_1, trace_out_2, trace_out_3))
    ]
    for departure in departures:
        departure.start()
    masks = block_masks()
    matrix = lobatto_matrix(POINTS - 1)
    mirrored = matrix[:, ::-1]
    odd_table = (matrix - mirrored)[:4, :3] / 2.0
    even_table = (matrix + mirrored)[:3, :3] / 2.0
    centre = matrix[:3, 3]

    def gather(chunk):
        for place, tile in enumerate(range(CHUNKS[chunk], CHUNKS[chunk + 1])):
            rows = slice(64 * place, 64 * place + 64)
            for half in range(2):
                swapped = gather_blocks([in_ref[8 * half + k, tile] for k in range(8)], masks)
                upper, lower = split_two(jnp.concatenate(swapped, axis=0))
                parts[chunk][rows, 128 * half : 128 * half + 128] = upper
                parts[chunk][rows, MODES + 128 * half : MODES + 128 * half + 128] = lower

    def synthesize(half, chunk):
        both = parts[chunk][...]
        deep = jnp.concatenate([both, both[:, :MODES]], axis=1)
        rows = slice(64 * CHUNKS[chunk], 64 * CHUNKS[chunk + 1])
        lanes = slice(MODES * half, MODES * half + MODES)
        plane[rows, lanes] = dot(deep, synth_ref[:, lanes])

    def derive(half, field):
        source = slice(MODES * half, MODES * half + 128)
        lanes = slice(128 * half, 128 * half + 128)

        def at(point):
            row = (field * QUAD + point) * 8
            return slice(row, row + 8)

        for line in range(POINTS):
            for stride, base, target in ((1, 7 * line, first), (7, line, second)):
                values = [plane[at(base + stride * k), source] for k in range(POINTS)]
                for k, slope in enumerate(derive_line(values, odd_table, even_table, centre)):
                    target[at(base + stride * k), lanes] = slope

    def combine(half, point):
        east_first, north_first, east_second, north_second = (
            metric_ref[point * 4 + k] for k in range(4)
        )
        source = slice(MODES * half, MODES * half + 128)
        span = slice(MODES * half + 128, MODES * half + MODES)
        lanes = slice(128 * half, 128 * half + 128)

        def at(field):
            return pl.ds(pl.multiple_of((field * QUAD + point) * 8, 8), 8)

        speed = [plane[at(k), source] for k in range(3)]
        base = [plane[at(3 + k), source] for k in range(3)]
        along = sum(speed[k] * first[at(3 + k), lanes] for k in range(3))
        across = sum(speed[k] * second[at(3 + k), lanes] for k in range(3))
        turned = (
            east_first * along + east_second * across,
            north_first * along + north_second * across,
            sum(speed[k] * plane[at(3 + k), span] for k in range(3)),
        )
        flow_first = base[0] * east_first + base[1] * north_first
        flow_second = base[0] * east_second + base[1] * north_second
        for k in range(3):
            carried = (
                flow_first * first[at(k), lanes]
                + flow_second * second[at(k), lanes]
                + base[2] * plane[at(k), span]
            )
            product[at(k), lanes] = turned[k] - carried

    def analyse(chunk):
        rows = slice(64 * BACK_CHUNKS[chunk], 64 * BACK_CHUNKS[chunk + 1])
        upper, lower = split_two(product[rows, :])
        return dot(jnp.concatenate([upper, lower, upper], axis=1), back_ref[...])

    def scatter(chunk, coefficient):
        for place, tile in enumerate(range(BACK_CHUNKS[chunk], BACK_CHUNKS[chunk + 1])):
            for half in range(2):
                pieces = [
                    coefficient[64 * place + 8 * k : 64 * place + 8 * k + 8, 128 * half : 128 * half + 128]
                    for k in range(8)
                ]
                for k, swapped in enumerate(scatter_blocks(pieces, masks)):
                    out_ref[8 * half + k, tile] = swapped


    product[BACK_ROWS * 8 :, :] = jnp.zeros((BACK_TILES * 64 - BACK_ROWS * 8, MODES), jnp.float32)
    gather(0)
    for chunk in range(6):
        synthesize(0, chunk)
        if chunk < 5:
            gather(chunk + 1)
        if chunk:
            derive(0, chunk - 1)
    for chunk in range(6):
        synthesize(1, chunk)
        if chunk == 0:
            derive(0, 5)
        else:
            derive(1, chunk - 1)
    derive(1, 5)
    metric_copy.wait()
    for copy in back_copies:
        copy.wait()

    @pl.loop(0, QUAD, unroll=4)
    def _(point):
        combine(0, point)
        combine(1, point)
    held = analyse(0)
    for chunk in range(4):
        following = analyse(chunk + 1) if chunk < 3 else None
        scatter(chunk, held)
        held = following
        if chunk >= 2:
            first_tile = 0 if chunk == 2 else BACK_CHUNKS[3]
            tiles = pl.ds(first_tile, BACK_CHUNKS[chunk + 1] - first_tile)
            departures.append(
                pltpu.make_async_copy(
                    out_ref.at[:, tiles], out_hbm.at[:, tiles], out_sems.at[2 + chunk]
                )
            )
            departures[-1].start()
    for departure in departures:
        departure.wait()


def traces_of(adjoint_ref):
    return jnp.concatenate(
        [
            jnp.concatenate(
                [adjoint_ref[component * QUAD + rim_point(side, step)] for side in range(4)], axis=1
            )
            for component in range(3)
            for step in range(POINTS)
        ],
        axis=0,
    )


def outgoing_traces(adjoint_ref, sides_ref, out_ref):
    sides = jnp.concatenate([sides_ref[d : d + 1] for d in range(4)], axis=1)
    chosen = lax.broadcasted_iota(jnp.int32, (512, 4 * SLOTS), 0) == sides
    chosen = jnp.where(chosen, 1.0, 0.0).astype(jnp.bfloat16)
    outgoing = sum(dot(part, chosen) for part in split_three(traces_of(adjoint_ref)))
    padding = jnp.zeros((TRACE_LANES - TRACE_ROWS, 128), jnp.float32)
    out_ref[...] = jnp.concatenate([outgoing, padding], axis=0).T


def stack_table(source, target, sems):
    copies = [
        pltpu.make_async_copy(
            source.at[pl.ds(MODES * part, MODES)],
            target.at[pl.ds(MODES * place, MODES)],
            sems.at[place],
        )
        for place, part in enumerate((0, 0, 1))
    ]
    for copy in copies:
        copy.start()
    return copies


def spread_metric(group_ref, metric_ref, turned, spread):
    rows = [metric_ref[point] for point in range(QUAD)]
    turned[...] = jnp.concatenate(
        rows + [jnp.zeros((256 - 4 * QUAD, 128), jnp.float32)], axis=0
    ).T
    own = turned[pl.ds(pl.multiple_of(group_ref[0] * NEAR, NEAR), NEAR), :]
    for index in range(4 * QUAD):
        spread[index] = jnp.broadcast_to(own[:, index : index + 1], (NEAR, 128))


def jump_kernel(adjoint_hbm, index_ref, penalty_ref, *refs):
    received_refs, (out_ref, adjoint_ref, sem) = refs[:4], refs[4:]
    copy = pltpu.make_async_copy(adjoint_hbm, adjoint_ref, sem)
    copy.start()
    received = jnp.concatenate([ref[...] for ref in received_refs], axis=0).T[:TRACE_ROWS]
    copy.wait()
    traces = traces_of(adjoint_ref)
    index = index_ref[...]
    where_local = lax.broadcasted_iota(jnp.int32, (512, 128), 0)
    where_far = lax.broadcasted_iota(jnp.int32, (128, 128), 0) + 512
    local_parts = split_three(traces)
    far_parts = split_three(received)
    for side in range(4):
        wanted = index[side : side + 1]
        near = jnp.where(where_local == wanted, 1.0, 0.0).astype(jnp.bfloat16)
        far = jnp.where(where_far == wanted, 1.0, 0.0).astype(jnp.bfloat16)
        outer = sum(dot(part, near) for part in local_parts) + sum(
            dot(part, far) for part in far_parts
        )
        for component in range(3):
            for step in range(POINTS):
                row = (component * POINTS + step) * GROUPS
                far_row = (component * POINTS + 6 - step) * GROUPS
                weight = penalty_ref[side * POINTS + step : side * POINTS + step + 1]
                inner = adjoint_ref[component * QUAD + rim_point(side, step)]
                jump = outer[far_row : far_row + GROUPS] - inner
                out_ref[(component * POINTS + step) * 4 + side] = weight * jump


BACK_GROUPS = (0, 7, 13, BACK_TILES)


def unpack_kernel(group_ref, in_ref, jump_ref, out_ref, advect, sems):
    turn = group_ref[0] % 8
    sides_at = {}
    for side in range(4):
        for step in range(POINTS):
            sides_at.setdefault(rim_point(side, step), []).append((side, step))
    departures = []
    for component in range(3):
        for tile in range(BACK_GROUPS[component], BACK_GROUPS[component + 1]):
            block = in_ref[:, tile].reshape(128, 128).T
            for k in range(8):
                row = 8 * tile + lax.rem(k - turn + 8, 8)
                advect[row] = block[16 * k : 16 * k + 16]
        first = component * QUAD
        for point, sides in sides_at.items():
            value = advect[first + point]
            for side, step in sides:
                value = value + jump_ref[(component * POINTS + step) * 4 + side]
            advect[first + point] = value
        departures.append(
            pltpu.make_async_copy(
                advect.at[pl.ds(first, QUAD)], out_ref.at[pl.ds(first, QUAD)], sems.at[component]
            )
        )
        departures[-1].start()
    for departure in departures:
        departure.wait()


def call(kernel, outs, *args, places=None, scratch=(), grant=12):
    spaces = {"v": pltpu.VMEM, "V": pltpu.VMEM, "h": pltpu.HBM, "s": pltpu.SMEM}
    places = places or "v" * len(args)
    many = isinstance(outs, list)
    outs = [
        jax.ShapeDtypeStruct(o, jnp.float32) if isinstance(o, tuple) else o
        for o in (outs if many else [outs])
    ]
    out_specs = [
        pl.BlockSpec(memory_space=getattr(o, "memory_space", None) or pltpu.VMEM) for o in outs
    ]
    moved = sum(int(np.prod(a.shape)) * a.dtype.itemsize for a in (*args, *outs))
    args = [
        pltpu.with_memory_space_constraint(a, spaces[p]) if p in "hV" else a
        for a, p in zip(args, places)
    ]
    return pl.pallas_call(
        kernel,
        out_shape=outs if many else outs[0],
        in_specs=[pl.BlockSpec(memory_space=spaces[p]) for p in places],
        out_specs=out_specs if many else out_specs[0],
        scratch_shapes=list(scratch),
        compiler_params=pltpu.CompilerParams(vmem_limit_bytes=grant * MEBI),
        cost_estimate=pl.CostEstimate(flops=0, bytes_accessed=moved, transcendentals=0),
    )(*args)


def passed_along(block, axis, distance):
    count = lax.axis_size(axis)
    return lax.ppermute(block, axis, [((i - distance) % count, i) for i in range(count)])


def shards(adjoint, base_flow, metric, penalty, send_sides, ext_index):
    synthesis, analysis, slope = fourier_tables()
    by_half = np.arange(2 * MODES).reshape(2, 2, 128).transpose(1, 0, 2).reshape(-1)
    synth = stacked(np.concatenate([synthesis, slope], axis=0)[by_half].T)
    back = stacked(analysis.T)
    natural = jnp.transpose(adjoint, (0, 2, 1, 3)).reshape(BACK_ROWS, GROUPS, 128)
    base = jnp.transpose(base_flow, (0, 2, 1, 3)).reshape(BACK_ROWS, GROUPS, 128)
    group = lax.axis_index("mode").reshape(1)

    f32, bf16 = jnp.float32, jnp.bfloat16
    packed, traces, own_metric, synth = call(
        pack_kernel,
        [
            pltpu.HBM((GROUPS, FIELD_TILES, NEAR, 128), f32),
            (4 * SLOTS, TRACE_LANES),
            pltpu.HBM((4 * QUAD, NEAR, 128), f32),
            pltpu.VMEM((3 * MODES, 2 * MODES), bf16),
        ],
        group,
        natural,
        base,
        send_sides.reshape(4, SLOTS),
        jnp.transpose(metric, (1, 0, 2)),
        jnp.asarray(synth),
        places="shhhhh",
        scratch=[
            pltpu.VMEM((8 * FIELD_TILES, GROUPS, 128), f32),
            pltpu.VMEM((GROUPS, FIELD_TILES, NEAR, 128), f32),
            pltpu.VMEM((128, 256), f32),
            pltpu.VMEM((4 * QUAD, NEAR, 128), f32),
            pltpu.VMEM((4, SLOTS), jnp.int32),
            pltpu.VMEM((QUAD, 4, 128), f32),
            pltpu.SemaphoreType.DMA((7,)),
            pltpu.SemaphoreType.DMA((7,)),
            pltpu.SemaphoreType.DMA((6,)),
        ],
        grant=16,
    )
    arrived = lax.all_to_all(packed, "mode", split_axis=0, concat_axis=0, tiled=True)
    coefficients, *outgoing = call(
        main_kernel,
        [pltpu.HBM((GROUPS, BACK_TILES, NEAR, 128), f32)]
        + [pltpu.HBM((SLOTS, TRACE_LANES), f32)] * 4,
        arrived,
        own_metric,
        synth,
        jnp.asarray(back),
        traces,
        places="Vhvhh",
        scratch=[
            pltpu.VMEM((4 * QUAD, NEAR, 128), f32),
            pltpu.VMEM((3 * MODES, MODES), bf16),
            pltpu.VMEM((GROUPS, BACK_TILES, NEAR, 128), f32),
            pltpu.SemaphoreType.DMA((4,)),
            pltpu.SemaphoreType.DMA((6,)),
            pltpu.VMEM((64 * FIELD_TILES, 2 * MODES), f32),
            pltpu.VMEM((8 * ROWS, MODES), f32),
            pltpu.VMEM((8 * ROWS, MODES), f32),
            pltpu.VMEM((64 * BACK_TILES, MODES), f32),
        ]
        + [
            pltpu.VMEM((64 * (end - first), 2 * MODES), bf16)
            for first, end in zip(CHUNKS, CHUNKS[1:])
        ],
        grant=28,
    )
    returned = lax.all_to_all(coefficients, "mode", split_axis=0, concat_axis=0, tiled=True)
    received = [passed_along(block, "elem", o) for block, o in zip(outgoing, OFFSETS)]
    jumps = call(
        jump_kernel,
        (84, GROUPS, 128),
        natural,
        ext_index,
        penalty.reshape(4 * POINTS, 128),
        *received,
        places="hvvvvvv",
        scratch=[pltpu.VMEM((BACK_ROWS, GROUPS, 128), f32), pltpu.SemaphoreType.DMA(())],
    )
    out = call(
        unpack_kernel,
        pltpu.HBM((BACK_ROWS, GROUPS, 128), jnp.float32),
        group,
        returned,
        jumps,
        places="svv",
        scratch=[
            pltpu.VMEM((8 * BACK_TILES, GROUPS, 128), f32),
            pltpu.SemaphoreType.DMA((3,)),
        ],
    )
    return jnp.transpose(out.reshape(3, QUAD, GROUPS, 128), (0, 2, 1, 3))


def solution(mesh):
    placed = (
        P(None, "mode", None, "elem"),
        P(None, "mode", None, "elem"),
        P(None, None, "elem"),
        P(None, None, "elem"),
        P("elem", None, None),
        P(None, "elem"),
    )
    return jax.shard_map(
        shards, mesh=mesh, in_specs=placed, out_specs=P(None, "mode", None, "elem"), check_vma=False
    )
```
